512 devices in a mesh: lat: 16 (over x, y_lo, core), lon: 32 (over y_hi, z).
Axes of the slice: x: 4, y: 4 (y_hi: 2, y_lo: 2; y = y_hi * 2 + y_lo), z: 16, core: 2. Of those that a mesh axis runs over, the one named last changes fastest.
Arguments:
- tokens: bfloat16 [4, 96, 384, 384], P(None, 'lat', 'lon'), may hold values from -6 to 6
- position_index: int32 [144, 144], replicated, may hold values from 0 to 3311
- gain_first: float32 [384], replicated, may hold values from 0.1 to 1.9
- qkv_first: bfloat16 [384, 1152], replicated, may hold values from -0.3125 to 0.3125
- proj_first: bfloat16 [384, 384], replicated, may hold values from -0.8984375 to 0.8984375
- bias_first: bfloat16 [16, 2, 12, 3312], P('lat'), may hold values from -4 to 4
- gain_second: float32 [384], replicated, may hold values from 0.1 to 1.9
- qkv_second: bfloat16 [384, 1152], replicated, may hold values from -0.3125 to 0.3125
- proj_second: bfloat16 [384, 384], replicated, may hold values from -0.8984375 to 0.8984375
- bias_second: bfloat16 [16, 2, 12, 3312], P('lat'), may hold values from -4 to 4
Outputs:
- mixed: bfloat16 [4, 96, 384, 384], P(None, 'lat', 'lon')
The draws below stay inside these ranges and needn't reach their ends.
All inputs are finite; a program needn't handle non-finite values.
Results may differ from the reference program's by a relative error of at most 0.015.
Values may be sent and summed in bfloat16 or wider, within the bound.
No kernel may reach another device: no remote copies, remote signals or barrier semaphores. Data moves between devices by JAX's collectives and lax.ppermute only.
A program may use at most 64 MiB of HBM per device.

```python
import jax
import jax.numpy as jnp
from jax import lax

HEADS = 12
D = 384
LEV = 4
POS = 3312
WIN = 144
LAT = 96
LON = 384
LATW = 16
LEVW = 2


def with_ends(entries, own_key, low, top_value):
    extent = entries.shape
    index_at = [jax.random.randint(jax.random.fold_in(own_key, axis), (), 0, extent[axis]) for axis in range(len(extent))]
    entries = entries.at[tuple(index_at)].set(low)
    longest = extent.index(max(extent))
    index_at[longest] = (index_at[longest] + 1) % extent[longest]
    return entries.at[tuple(index_at)].set(top_value)


def shard_levels(own_key, shape, pieces, smallest, top_value):
    def one(position, blocks):
        draws = jax.random.uniform(jax.random.fold_in(jax.random.fold_in(own_key, 6), position), (blocks,), jnp.float32, smallest / len(pieces), top_value / len(pieces))
        return jnp.repeat(jnp.exp(draws), shape[position] // blocks).reshape((-1,) + (1,) * (len(shape) - position - 1))

    level = one(*pieces[0])
    for cut in pieces[1:]:
        level = level * one(*cut)
    return level


def scatter_about(own_key, extent, scale, reach, pieces=(), kind=jnp.bfloat16):
    drawn = jax.random.normal(own_key, extent, jnp.float32) * scale
    if len(pieces) > 0:
        drawn = shard_levels(own_key, extent, pieces, -0.22, 0.18) * drawn
    return jnp.clip(drawn, min=-reach, max=reach).astype(kind)


def setup_inputs(seed: int = 0) -> dict:
    seeds = jax.random.split(jax.random.key(seed), 11)
    tokens = scatter_about(seeds[0], (LEV, LAT, LON, D), 1.0, 6.0, ((1, 16), (2, 32)))
    position_index = with_ends(jax.random.randint(seeds[1], (WIN, WIN), 0, POS), jax.random.fold_in(seeds[1], 1), 0, POS - 1).astype(jnp.int32)
    gain_first = jnp.clip(1.0 + 0.18 * jax.random.normal(seeds[2], (D,), jnp.float32), 0.1, 1.9)
    qkv_first = scatter_about(seeds[3], (D, 3 * D), D ** -0.5, 0.3125)
    proj_first = scatter_about(seeds[4], (D, D), 0.15, 0.8984375)
    bias_first = scatter_about(seeds[5], (LATW, LEVW, HEADS, POS), 1.0, 4.0, ((0, 16),))
    gain_second = jnp.clip(1.0 + 0.18 * jax.random.normal(seeds[6], (D,), jnp.float32), 0.1, 1.9)
    qkv_second = scatter_about(seeds[7], (D, 3 * D), D ** -0.5, 0.3125)
    proj_second = scatter_about(seeds[8], (D, D), 0.15, 0.8984375)
    bias_second = scatter_about(seeds[9], (LATW, LEVW, HEADS, POS), 1.0, 4.0, ((0, 16),))
    return dict(tokens=tokens, position_index=position_index, gain_first=gain_first, qkv_first=qkv_first, proj_first=proj_first, bias_first=bias_first, gain_second=gain_second, qkv_second=qkv_second, proj_second=proj_second, bias_second=bias_second)


def window_block(grid, valid, side, table, position_index, gain, w_qkv, w_proj):
    levels, rows, cols, width = grid.shape
    heads = table.shape[2]
    head_dim = width // heads
    rwin = rows // 6
    lwin = levels // 2
    cwin = cols // 12
    values = grid.astype(jnp.float32)
    center = lax.optimization_barrier(jnp.mean(values, axis=-1, keepdims=True))
    spread = lax.optimization_barrier(jnp.mean((values - center) ** 2, axis=-1, keepdims=True))
    normed = ((values - center) * lax.rsqrt(spread + 1e-05) * gain).astype(jnp.bfloat16)
    qkv = jnp.dot(normed.reshape(-1, width), w_qkv, preferred_element_type=jnp.float32).astype(jnp.bfloat16)
    qkv = qkv.reshape(lwin, 2, rwin, 6, cwin, 12, 3 * width).transpose(2, 0, 4, 1, 3, 5, 6)
    qkv = qkv.reshape(rwin, lwin, cwin, 144, 3 * width)
    val_win = jnp.broadcast_to(valid.reshape(rwin, 1, 1, 6, 1), (rwin, lwin, 2, 6, 12)).reshape(rwin, lwin, 144)
    side_win = jnp.broadcast_to(side.reshape(1, lwin, 2, 1, 1), (rwin, lwin, 2, 6, 12)).reshape(rwin, lwin, 144)
    same = side_win[..., :, None] == side_win[..., None, :]
    mask = same & val_win[..., None, :] | jnp.eye(144, dtype=bool)
    bias = jnp.take(table, position_index, axis=3)

    def one_row(args):
        block, bias_row, mask_row = args
        query = block[..., :width].reshape(lwin, cwin, 144, heads, head_dim).astype(jnp.float32)
        key = block[..., width:2 * width].reshape(lwin, cwin, 144, heads, head_dim).astype(jnp.float32)
        value = block[..., 2 * width:].reshape(lwin, cwin, 144, heads, head_dim).astype(jnp.float32)
        scores = jnp.einsum('lcqhd,lckhd->lchqk', query, key) * head_dim ** (-0.5)
        scores = scores + bias_row[:, None].astype(jnp.float32)
        expd = jnp.exp(jnp.where(mask_row[:, None, None], scores, -1e+30))
        probs = (expd / lax.optimization_barrier(jnp.sum(expd, axis=-1, keepdims=True))).astype(jnp.bfloat16)
        attended = jnp.einsum('lchqk,lckhd->lcqhd', probs.astype(jnp.float32), value)
        return attended.astype(jnp.bfloat16).reshape(lwin, cwin, 144, width)
    attended = lax.map(one_row, (qkv, bias, mask))
    attended = attended.reshape(rwin, lwin, cwin, 2, 6, 12, width).transpose(1, 3, 0, 4, 2, 5, 6)
    attended = attended.reshape(-1, width)
    update = jnp.dot(attended, w_proj, preferred_element_type=jnp.float32).reshape(values.shape)
    return (values + update).astype(jnp.bfloat16)

def reference(tokens, position_index, gain_first, qkv_first, proj_first, bias_first, gain_second, qkv_second, proj_second, bias_second):
    levels, rows, cols, width = tokens.shape
    first = window_block(tokens, jnp.ones((rows,), bool), jnp.zeros((levels,), bool), bias_first, position_index, gain_first, qkv_first, proj_first)
    rolled = jnp.roll(jnp.roll(first, -6, axis=2), -1, axis=0)
    ext = jnp.pad(rolled, ((0, 0), (3, 3), (0, 0), (0, 0)))
    row_ids = jnp.arange(rows + 6)
    valid = (row_ids >= 3) & (row_ids < rows + 3)
    side = jnp.arange(levels) == levels - 1
    table = jnp.concatenate([bias_second[0:1], bias_second], axis=0)
    second = window_block(ext, valid, side, table, position_index, gain_second, qkv_second, proj_second)
    second = second[:, 3:rows + 3]
    return jnp.roll(jnp.roll(second, 1, axis=0), 6, axis=2)
```

```python
import functools

import jax
import jax.numpy as jnp
import numpy as np
from jax import lax
from jax.experimental import pallas as pl
from jax.experimental.pallas import tpu as pltpu
from jax.sharding import PartitionSpec as P

F32, BF16, I32 = jnp.float32, jnp.bfloat16, jnp.int32
HEADS = 12
D = 384
WIN = 144
CHUNKS = 26
LOG2E = float(np.log2(np.e))
FIX = 8191.0
SCALE = LOG2E * 32 ** -0.5
UNFIX = LOG2E / FIX


def dot(a, b):
    return jnp.dot(a, b, preferred_element_type=F32)


def dot_t(a, b):
    return lax.dot_general(a, b, (((1,), (1,)), ((), ())), preferred_element_type=F32)


def one_hot_rows(rows, width):
    out = np.zeros((len(rows), width), np.float32)
    for i, r in enumerate(rows):
        if r >= 0:
            out[i, r] = 1
    return out.astype(jnp.bfloat16)


LEVEL = [[1, 2], [3, 0]]


def compact_from_padded():
    return one_hot_rows([g * 16 + c for g in range(24) for c in range(12)], 384)


def quadrants_from_compact():
    rows = []
    for b in range(2):
        for a in range(2):
            for w in range(2):
                for lo in range(2):
                    for r in range(3):
                        for c in range(6):
                            rows.append(LEVEL[w][lo] * 72 + (3 * a + r) * 12 + 6 * b + c)
    return one_hot_rows(rows, 288)


def keys_from_pieces():
    return one_hot_rows(
        [80 * piece + 36 * w + t for w in range(2) for piece in range(4) for t in range(36)], 320
    )


def queries_from_quadrants():
    rows = []
    for a in range(2):
        for b in range(2):
            for w in range(2):
                rows += [((b * 2 + a) * 2 + w) * 36 + t for t in range(36)] + [-1] * 4
    return one_hot_rows(rows, 288)


def padded_from_queries():
    rows = []
    for l in range(4):
        w, lo = [(1, 1), (0, 0), (0, 1), (1, 0)][l]
        for r in range(6):
            for c in range(16):
                if c >= 12:
                    rows.append(-1)
                    continue
                a, b = r // 3, c // 6
                rows.append(((a * 2 + b) * 2 + w) * 40 + lo * 18 + (r % 3) * 6 + c % 6)
    return one_hot_rows(rows, 320)


def tail_copies(columns):
    order = list(columns[:128]) + list(columns[128:]) * 8
    return np.ascontiguousarray(one_hot_rows(order, WIN).T)


def tail_rows(tiles):
    packed = -(-tiles // 8)
    out = np.zeros((packed * 8, tiles * 8), np.float32)
    for t in range(tiles):
        for s in range(8):
            out[(t // 8) * 8 + s, t * 8 + s] = 1
    return out.astype(jnp.bfloat16)


def shifted_positions(a, b):
    queries = [
        72 * lo + 12 * (3 * (1 - a) + r) + 6 * (1 - b) + c
        for lo in range(2)
        for r in range(3)
        for c in range(6)
    ]
    keys = []
    for near_row, near_col in ((1, 1), (1, 0), (0, 1), (0, 0)):
        row0 = 3 * (1 - a) if near_row else 3 * a
        col0 = 6 * (1 - b) if near_col else 6 * b
        keys += [
            72 * lo + 12 * (row0 + r) + col0 + c
            for lo in range(2)
            for r in range(3)
            for c in range(6)
        ]
    return queries, keys


def pack_table(top, bottom, packed_ref):
    first = jnp.round(top.astype(F32) * FIX).astype(I32)
    second = jnp.round(bottom.astype(F32) * FIX).astype(I32)
    packed_ref[:, 0 : top.shape[1]] = (first << 16) | (second & 0xFFFF)


def split_index(position_index):
    high = (position_index >> 7).astype(F32).astype(BF16)
    low = (position_index & 127).astype(F32).astype(BF16)
    return high, low


def fold_tail(values, gather_rows, tiles):
    row = lax.broadcasted_iota(I32, values.shape, 0) // 8
    lane = lax.broadcasted_iota(I32, values.shape, 1) // 16
    kept = jnp.where((row % 8) == lane, values, 0.0).astype(BF16)
    return dot(gather_rows, kept)


def place_index(part, columns, gather_rows, dst_ref, start, tiles):
    spread = dot(part, columns)
    rows = tiles * 8
    dst_ref[start : start + rows, :] = spread[:, :128].astype(I32)
    tail = fold_tail(spread[:, 128:], gather_rows, tiles)
    dst_ref[start + rows : start + rows + tail.shape[0], :] = tail.astype(I32)


def expand(packed_ref, high_ref, low_ref, out_ref, start, count):
    def tile(t, carry):
        rows = pl.ds(pl.multiple_of(start + t * 8, 8), 8)
        low = low_ref[rows, :]
        high = high_ref[rows, :]
        picked = [None] * HEADS
        for c in range(CHUNKS):
            here = high == c
            for h in range(HEADS):
                entries = jnp.broadcast_to(packed_ref[h : h + 1, 128 * c : 128 * c + 128], (8, 128))
                got = jnp.take_along_axis(entries, low, axis=1, mode="promise_in_bounds")
                picked[h] = got if c == 0 else jnp.where(here, got, picked[h])
        for h in range(HEADS):
            out_ref[h, rows, :] = picked[h]
        return carry

    lax.fori_loop(0, count, tile, 0)


def bias_tail(bias_ref, h, base, tiles):
    out = []
    for t in range(tiles):
        at = base + (t // 8) * 8
        part = bias_ref[h, at : at + 8, :]
        j = t % 8
        out.append(part if j == 0 else pltpu.roll(part, 128 - 16 * j, 1))
    return jnp.concatenate(out, axis=0)


def upper(packed):
    return (packed >> 16).astype(F32)


def lower(packed):
    return ((packed << 16) >> 16).astype(F32)


def layer_norm(values, gain):
    center = jnp.mean(values, axis=-1, keepdims=True)
    moved = values - center
    spread = jnp.mean(moved * moved, axis=-1, keepdims=True)
    return (moved * lax.rsqrt(spread + 1e-05) * gain).astype(BF16)


def head_masks(shape):
    lane = lax.broadcasted_iota(I32, shape, 1) // 32
    return [lane == i for i in range(4)]


def softmax(scores, mask):
    raised = jnp.where(mask, jnp.exp2(scores), 0.0)
    total = jnp.sum(raised, axis=-1, keepdims=True)
    step = jnp.where(total > 1.0, 0.25, 1.0)
    return ((raised * step) * (1.0 / (total * step))).astype(BF16)


def first_kernel(
    tok_ref, idx_ref, gain_ref, wqkv_ref, wo_ref, table_ref, gain2_ref,
    perm_ref, quad_ref, cols_ref, tailrows_ref,
    first_ref, west_ref, east_ref,
    padded, packed, high_ref, low_ref, bias_ref, kpad, vpad,
):
    pack_table(table_ref[0, 0], table_ref[0, 1], packed)
    high, low = split_index(idx_ref[...])
    place_index(high, cols_ref[...], tailrows_ref[...], high_ref, 0, 18)
    place_index(low, cols_ref[...], tailrows_ref[...], low_ref, 0, 18)
    expand(packed, high_ref, low_ref, bias_ref, 0, 21)

    padded[...] = jnp.zeros_like(padded)
    for g in range(24):
        padded[16 * g : 16 * g + 12, :] = tok_ref[g]
    values = dot(perm_ref[...], padded[...])
    normed = layer_norm(values, gain_ref[...])
    qkv = dot(normed, wqkv_ref[...]).astype(BF16)

    kpad[...] = jnp.zeros_like(kpad)
    vpad[...] = jnp.zeros_like(vpad)
    for w in range(2):
        rows = slice(WIN * w, WIN * w + WIN)
        kpad[w, 0:WIN, :] = qkv[rows, D : 2 * D]
        vpad[w, 0:WIN, :] = qkv[rows, 2 * D :]

    qmasks = head_masks((WIN, 128))
    vmasks = head_masks((256, 128))
    valid = lax.broadcasted_iota(I32, (WIN, 256), 1) < WIN
    zero = jnp.zeros((), BF16)
    mixed = [[None] * 3, [None] * 3]
    for g in range(3):
        lanes = slice(128 * g, 128 * g + 128)
        biases = []
        for i in range(4):
            h = 4 * g + i
            biases.append(
                jnp.concatenate([bias_ref[h, 0:WIN, :], bias_tail(bias_ref, h, WIN, 18)], axis=1)
            )
        for w in range(2):
            query = qkv[WIN * w : WIN * w + WIN, lanes]
            key = kpad[w, :, lanes]
            value = vpad[w, :, lanes]
            total = None
            for i in range(4):
                scores = dot_t(jnp.where(qmasks[i], query, zero), key)
                bias = upper(biases[i]) if w == 0 else lower(biases[i])
                probs = softmax(scores * SCALE + bias * UNFIX, valid)
                part = dot(probs, jnp.where(vmasks[i], value, zero))
                total = part if total is None else total + part
            mixed[w][g] = total.astype(BF16)
    attended = jnp.concatenate([jnp.concatenate(row, axis=1) for row in mixed], axis=0)
    first = (values + dot(attended, wo_ref[...])).astype(BF16)
    first_ref[...] = first
    again = layer_norm(first.astype(F32), gain2_ref[...])
    parts = dot(quad_ref[...], again).astype(BF16)
    for a in range(2):
        west_ref[a] = parts[72 * a : 72 * a + 72]
        east_ref[a] = parts[144 + 72 * a : 144 + 72 * a + 72]


SIDE_ROWS = 80
SIDE_TILES = 12


def bias_kernel(
    idx_ref, table_ref, before_ref, pick_ref, cols_ref, tailrows_ref,
    bias_ref,
    packed, high_ref, low_ref,
):
    pack_table(before_ref[0, 0], before_ref[0, 1], packed.at[0])
    pack_table(table_ref[0, 0], table_ref[0, 1], packed.at[1])
    high, low = split_index(idx_ref[...])
    for part, dst in ((high, high_ref), (low, low_ref)):
        rows = dot(pick_ref[...], part).astype(BF16)
        for a in range(2):
            spread = jnp.concatenate(
                [
                    dot(rows[40 * q : 40 * q + 40], cols_ref[q])
                    for q in (2 * a, 2 * a + 1)
                ],
                axis=0,
            )
            start = a * 96
            dst[start : start + 80, :] = spread[:, :128].astype(I32)
            tail = fold_tail(spread[:, 128:], tailrows_ref[...], 10)
            dst[start + 80 : start + 96, :] = tail.astype(I32)
    for a in range(2):
        expand(packed.at[a], high_ref, low_ref, bias_ref, a * 96, SIDE_TILES)


def second_kernel(
    edge_ref,
    first_ref, west_ref, east_ref, from_west_ref, from_east_ref, north_ref, south_ref,
    wqkv_ref, wo_ref, bias_ref,
    keys_ref, queries_ref, unperm_ref, pad_ref,
    out_ref,
    cat, qbuf, kpad, vpad, obuf,
):
    own = (west_ref, east_ref)
    beside = (from_west_ref, from_east_ref)
    beyond = (north_ref, south_ref)
    tokens = jnp.concatenate([west_ref[0], west_ref[1], east_ref[0], east_ref[1]], axis=0)
    asked = dot(queries_ref[...], tokens).astype(BF16)
    qbuf[...] = dot(asked, wqkv_ref[:, 0:D]).astype(BF16).astype(F32)

    cat[...] = jnp.zeros_like(cat)
    kpad[...] = jnp.zeros_like(kpad)
    vpad[...] = jnp.zeros_like(vpad)
    for a in range(2):
        for b in range(2):
            q = 2 * a + b
            far = ((1, 0), (2, 3))[b]
            cat[q, 0:72, :] = own[b][a]
            cat[q, 80:152, :] = beside[b][a]
            cat[q, 160:232, :] = beyond[a][far[0]]
            cat[q, 240:312, :] = beyond[a][far[1]]
            window = dot(keys_ref[...], cat[q]).astype(BF16)
            kv = dot(window, wqkv_ref[:, D:]).astype(BF16)
            for w in range(2):
                rows = slice(WIN * w, WIN * w + WIN)
                kpad[2 * q + w, 0:WIN, :] = kv[rows, 0:D]
                vpad[2 * q + w, 0:WIN, :] = kv[rows, D:]

    shape = (40, 256)
    lane = lax.broadcasted_iota(I32, shape, 1)
    side_q = jnp.minimum(lax.broadcasted_iota(I32, shape, 0) // 18, 1)
    side_k = (lane % 36) // 18
    inside = lane < WIN
    near = lane < 72
    split = side_q == side_k
    masks = {}
    for a in range(2):
        open_side = edge_ref[a] > 0
        for w in range(2):
            m = jnp.logical_and(inside, jnp.logical_or(near, open_side))
            masks[a, w] = jnp.logical_and(m, split) if w == 1 else m

    qmasks = head_masks((40, 128))
    vmasks = head_masks((256, 128))
    zero = jnp.zeros((), BF16)
    for g in range(3):
        lanes = slice(128 * g, 128 * g + 128)
        for a in range(2):
            biases = []
            for i in range(4):
                h = 4 * g + i
                biases.append(
                    jnp.concatenate(
                        [bias_ref[h, 96 * a : 96 * a + 80, :], bias_tail(bias_ref, h, 96 * a + 80, 10)],
                        axis=1,
                    )
                )
            for b in range(2):
                for w in range(2):
                    at = 4 * a + 2 * b + w
                    query = qbuf[40 * at : 40 * at + 40, lanes]
                    key = kpad[at, :, lanes]
                    value = vpad[at, :, lanes]
                    total = None
                    for i in range(4):
                        scores = dot_t(jnp.where(qmasks[i], query, 0.0).astype(BF16), key)
                        bias = biases[i][40 * b : 40 * b + 40]
                        bias = upper(bias) if w == 0 else lower(bias)
                        probs = softmax(scores * SCALE + bias * UNFIX, masks[a, w])
                        part = dot(probs, jnp.where(vmasks[i], value, zero))
                        total = part if total is None else total + part
                    obuf[40 * at : 40 * at + 40, lanes] = total
    attended = dot(unperm_ref[...], obuf[...].astype(BF16)).astype(BF16)
    result = dot(pad_ref[...], first_ref[...]) + dot(attended, wo_ref[...])
    result = result.astype(BF16)
    for g in range(24):
        out_ref[g] = result[16 * g : 16 * g + 12]


VMEM = pl.BlockSpec(memory_space=pltpu.VMEM)
SMEM = pl.BlockSpec(memory_space=pltpu.SMEM)
LIMIT = 48 * 1024 * 1024


def shift(block, axis, by, wrap):
    size = lax.axis_size(axis)
    route = [(i, (i + by) % size) for i in range(size) if wrap or 0 <= i + by < size]
    return lax.ppermute(block, axis, route)


def shards(
    tokens, position_index, gain_first, qkv_first, proj_first, bias_first,
    gain_second, qkv_second, proj_second, bias_second,
):
    lat = lax.axis_index("lat")
    last = lax.axis_size("lat") - 1
    tables_before = shift(bias_second, "lat", 1, False)
    tables_before = jnp.where(lat == 0, bias_second, tables_before)

    perm = compact_from_padded()
    first, west, east = pl.pallas_call(
        first_kernel,
        out_shape=(
            jax.ShapeDtypeStruct((288, D), BF16),
            jax.ShapeDtypeStruct((2, 72, D), BF16),
            jax.ShapeDtypeStruct((2, 72, D), BF16),
        ),
        in_specs=[VMEM] * 11,
        out_specs=(VMEM,) * 3,
        scratch_shapes=[
            pltpu.VMEM((384, D), BF16),
            pltpu.VMEM((HEADS, CHUNKS * 128), I32),
            pltpu.VMEM((168, 128), I32),
            pltpu.VMEM((168, 128), I32),
            pltpu.VMEM((HEADS, 168, 128), I32),
            pltpu.VMEM((2, 256, D), BF16),
            pltpu.VMEM((2, 256, D), BF16),
        ],
        compiler_params=pltpu.CompilerParams(vmem_limit_bytes=LIMIT),
        cost_estimate=pl.CostEstimate(flops=10**9, bytes_accessed=3 * 10**6, transcendentals=10**6),
        name="first_block",
    )(
        tokens.reshape(24, 12, D), position_index, gain_first.reshape(1, D), qkv_first, proj_first,
        bias_first, gain_second.reshape(1, D),
        jnp.asarray(perm), jnp.asarray(quadrants_from_compact()),
        jnp.asarray(tail_copies(list(range(WIN)))), jnp.asarray(tail_rows(18)),
    )

    from_west = shift(east, "lon", 1, True)
    from_east = shift(west, "lon", -1, True)

    picks = np.zeros((160, WIN), np.float32).astype(jnp.bfloat16)
    columns = []
    for a in range(2):
        for b in range(2):
            queries, keys = shifted_positions(a, b)
            q = 2 * a + b
            picks[40 * q : 40 * q + 36] = one_hot_rows(queries, WIN)
            columns.append(tail_copies(keys))
    bias = pl.pallas_call(
        bias_kernel,
        out_shape=jax.ShapeDtypeStruct((HEADS, 192, 128), I32),
        in_specs=[VMEM] * 6,
        out_specs=VMEM,
        scratch_shapes=[
            pltpu.VMEM((2, HEADS, CHUNKS * 128), I32),
            pltpu.VMEM((192, 128), I32),
            pltpu.VMEM((192, 128), I32),
        ],
        compiler_params=pltpu.CompilerParams(vmem_limit_bytes=LIMIT),
        cost_estimate=pl.CostEstimate(flops=10**9, bytes_accessed=10 * 10**6, transcendentals=10**6),
        name="second_bias",
    )(
        position_index, bias_second, tables_before,
        jnp.asarray(picks), jnp.asarray(np.stack(columns)), jnp.asarray(tail_rows(10)),
    )

    up = jnp.stack([from_west[0], west[0], east[0], from_east[0]])
    down = jnp.stack([from_west[1], west[1], east[1], from_east[1]])
    south = shift(up, "lat", -1, False)
    north = shift(down, "lat", 1, False)

    edges = jnp.stack([lat > 0, lat < last]).astype(I32)
    out = pl.pallas_call(
        second_kernel,
        out_shape=jax.ShapeDtypeStruct((24, 12, D), BF16),
        in_specs=[SMEM] + [VMEM] * 14,
        out_specs=VMEM,
        scratch_shapes=[
            pltpu.VMEM((4, 320, D), BF16),
            pltpu.VMEM((320, D), F32),
            pltpu.VMEM((8, 256, D), BF16),
            pltpu.VMEM((8, 256, D), BF16),
            pltpu.VMEM((320, D), F32),
        ],
        compiler_params=pltpu.CompilerParams(vmem_limit_bytes=LIMIT),
        cost_estimate=pl.CostEstimate(flops=10**9, bytes_accessed=5 * 10**6, transcendentals=10**6),
        name="second_block",
    )(
        edges, first, west, east, from_west, from_east, north, south,
        qkv_second, proj_second, bias,
        jnp.asarray(keys_from_pieces()), jnp.asarray(queries_from_quadrants()),
        jnp.asarray(padded_from_queries()), jnp.asarray(np.ascontiguousarray(perm.T)),
    )
    return out.reshape(4, 6, 12, D)


def solution(mesh):
    return jax.shard_map(
        shards,
        mesh=mesh,
        in_specs=(
            P(None, "lat", "lon", None), P(), P(), P(), P(),
            P("lat", None, None, None), P(), P(), P(), P("lat", None, None, None),
        ),
        out_specs=P(None, "lat", "lon", None),
        check_vma=False,
    )
```

```python
import jax
import jax.numpy as jnp
import numpy as np
from jax import lax
from jax.experimental import pallas as pl
from jax.experimental.pallas import tpu as pltpu
from jax.sharding import PartitionSpec as P

F32, BF16, I32 = jnp.float32, jnp.bfloat16, jnp.int32
HEADS = 12
D = 384
WIN = 144
CHUNKS = 26
POS = 3312
LOG2E = float(np.log2(np.e))
FIX = 8191.0
SCALE = LOG2E * 32 ** -0.5
UNFIX = LOG2E / FIX


def dot(a, b):
    return jnp.dot(a, b, preferred_element_type=F32)


def dot_t(a, b):
    return lax.dot_general(a, b, (((1,), (1,)), ((), ())), preferred_element_type=F32)


def one_hot(source, width):
    lane = lax.broadcasted_iota(I32, (source.shape[0], width), 1)
    return jnp.where(lane == source, 1.0, 0.0).astype(BF16)


def row_ids(count):
    return lax.broadcasted_iota(I32, (count, 1), 0)


def quadrants_from_natural():
    i = row_ids(288)
    b, a, w, lo = i // 144, i // 72 % 2, i // 36 % 2, i // 18 % 2
    level = (2 * w + lo + 1) % 4
    return one_hot(level * 72 + (3 * a + i // 6 % 3) * 12 + 6 * b + i % 6, 288)


def keys_from_pieces():
    i = row_ids(288)
    w, piece, t = i // 144, i // 36 % 4, i % 36
    return one_hot(80 * piece + 36 * w + t, 320)


def queries_from_quadrants():
    i = row_ids(320)
    a, b, w, t = i // 160, i // 80 % 2, i // 40 % 2, i % 40
    return one_hot(jnp.where(t < 36, b * 144 + a * 72 + w * 36 + t, -1), 288)


def natural_from_given():
    i = row_ids(288)
    return one_hot(i % 72 * 4 + i // 72, 288)


def given_from_natural():
    i = row_ids(288)
    return one_hot(i % 4 * 72 + i // 4, 288)


def given_from_queries():
    i = row_ids(288)
    level, r, c = (i % 4 + 3) % 4, i // 48, i // 4 % 12
    a, b, w, lo = r // 3, c // 6, level // 2, level % 2
    return one_hot(a * 160 + b * 80 + w * 40 + lo * 18 + r % 3 * 6 + c % 6, 320)


def tail_rows(tiles):
    packed = -(-tiles // 8) * 8
    shape = (packed, tiles * 8)
    i = lax.broadcasted_iota(I32, shape, 0)
    k = lax.broadcasted_iota(I32, shape, 1)
    take = jnp.logical_and(i // 8 == k // 64, i % 8 == k % 8)
    return jnp.where(take, 1.0, 0.0).astype(BF16)


def tail_columns():
    shape = (WIN, 256)
    i = lax.broadcasted_iota(I32, shape, 0)
    k = lax.broadcasted_iota(I32, shape, 1)
    return jnp.where(i == jnp.where(k < 128, k, 128 + k % 16), 1.0, 0.0).astype(BF16)


def shifted_query(a, b, i):
    return 72 * (i // 18) + 12 * (3 * (1 - a) + i // 6 % 3) + 6 * (1 - b) + i % 6


def shifted_key(a, b, i):
    piece, t = i // 36, i % 36
    row = jnp.where(piece < 2, 3 * (1 - a), 3 * a)
    col = jnp.where(piece % 2 == 0, 6 * (1 - b), 6 * b)
    return 72 * (t // 18) + 12 * (row + t // 6 % 3) + col + t % 6


def query_picks():
    i = row_ids(160)
    a, b, t = i // 80, i // 40 % 2, i % 40
    return one_hot(jnp.where(t < 36, shifted_query(a, b, t), -1), WIN)


def key_columns(a, b):
    k = lax.broadcasted_iota(I32, (1, 256), 1)
    position = shifted_key(a, b, jnp.where(k < 128, k, 128 + k % 16))
    i = lax.broadcasted_iota(I32, (WIN, 256), 0)
    return jnp.where(i == position, 1.0, 0.0).astype(BF16)


def pack_table(table_ref, packed_ref):
    for h in range(HEADS):
        fixed = jnp.round(table_ref[h].astype(F32) * FIX).astype(I32)
        packed_ref[h : h + 1, 0:POS] = (fixed[0:1] << 16) | (fixed[1:2] & 0xFFFF)


def split_index(position_index):
    high = (position_index >> 7).astype(F32).astype(BF16)
    low = (position_index & 127).astype(F32).astype(BF16)
    return high, low


def fold_tail(values, gather_rows, tiles):
    row = lax.broadcasted_iota(I32, values.shape, 0) // 8
    lane = lax.broadcasted_iota(I32, values.shape, 1) // 16
    kept = jnp.where((row % 8) == lane, values, 0.0).astype(BF16)
    return dot(gather_rows, kept)


def place_index(part, columns, gather_rows, dst_ref, start, tiles):
    spread = dot(part, columns)
    rows = tiles * 8
    dst_ref[start : start + rows, :] = spread[:, :128].astype(I32)
    tail = fold_tail(spread[:, 128:], gather_rows, tiles)
    dst_ref[start + rows : start + rows + tail.shape[0], :] = tail.astype(I32)


def expand(packed_ref, high_ref, low_ref, out_ref, start, count):
    def tile(t, carry):
        rows = pl.ds(pl.multiple_of(start + t * 8, 8), 8)
        low = low_ref[rows, :]
        high = high_ref[rows, :]
        picked = [None] * HEADS
        for c in range(CHUNKS):
            here = high == c
            for h in range(HEADS):
                entries = jnp.broadcast_to(packed_ref[h : h + 1, 128 * c : 128 * c + 128], (8, 128))
                got = jnp.take_along_axis(entries, low, axis=1, mode="promise_in_bounds")
                picked[h] = got if c == 0 else jnp.where(here, got, picked[h])
        for h in range(HEADS):
            out_ref[h, rows, :] = picked[h]
        return carry

    lax.fori_loop(0, count, tile, 0)


def bias_tail(bias_ref, h, base, tiles):
    out = []
    for t in range(tiles):
        at = base + (t // 8) * 8
        part = bias_ref[h, at : at + 8, :]
        j = t % 8
        out.append(part if j == 0 else pltpu.roll(part, 128 - 16 * j, 1))
    return jnp.concatenate(out, axis=0)


def upper(packed):
    return (packed >> 16).astype(F32)


def lower(packed):
    return ((packed << 16) >> 16).astype(F32)


def layer_norm(values, gain):
    center = jnp.mean(values, axis=-1, keepdims=True)
    moved = values - center
    spread = jnp.mean(moved * moved, axis=-1, keepdims=True)
    return (moved * lax.rsqrt(spread + 1e-05) * gain).astype(BF16)


def softmax(scores, mask):
    raised = jnp.where(mask, jnp.exp2(scores), 0.0)
    total = jnp.sum(raised, axis=-1, keepdims=True)
    step = jnp.where(total > 1.0, 0.25, 1.0)
    return ((raised * step) * (1.0 / (total * step))).astype(BF16)


def four_heads(query, key, value, biases, mask):
    n = query.shape[0]
    own = lax.broadcasted_iota(I32, query.shape, 1) // 32
    stacked = jnp.concatenate([jnp.where(own == i, query, 0.0) for i in range(4)], axis=0)
    scores = dot_t(stacked.astype(BF16), key)
    probs = [
        softmax(scores[n * i : n * i + n] * SCALE + biases[i] * UNFIX, mask) for i in range(4)
    ]
    parts = dot(jnp.concatenate(probs, axis=0), value)
    out = parts[0:n]
    for i in range(1, 4):
        out = jnp.where(own == i, parts[n * i : n * i + n], out)
    return out


def first_kernel(
    tok_ref, idx_ref, gain_ref, wqkv_ref, wo_ref, table_ref, gain2_ref,
    first_ref, west_ref, east_ref,
    values_ref, packed, high_ref, low_ref, bias_ref, qbuf, kpad, vpad, obuf,
):
    pack_table(table_ref, packed)
    high, low = split_index(idx_ref[...])
    columns, gather_rows = tail_columns(), tail_rows(18)
    place_index(high, columns, gather_rows, high_ref, 0, 18)
    place_index(low, columns, gather_rows, low_ref, 0, 18)
    expand(packed, high_ref, low_ref, bias_ref, 0, 21)

    for g in range(72):
        values_ref[4 * g : 4 * g + 4, :] = tok_ref[g].astype(F32)
    values = dot(natural_from_given(), values_ref[...].astype(BF16))
    values_ref[...] = values
    normed = layer_norm(values, gain_ref[...])
    qkv = dot(normed, wqkv_ref[...]).astype(BF16)
    qbuf[...] = qkv[:, 0:D].astype(F32)
    for w in range(2):
        rows = slice(WIN * w, WIN * w + WIN)
        kpad[w, 0:WIN, :] = qkv[rows, D : 2 * D]
        vpad[w, 0:WIN, :] = qkv[rows, 2 * D :]
        kpad[w, WIN:, :] = jnp.zeros((256 - WIN, D), BF16)
        vpad[w, WIN:, :] = jnp.zeros((256 - WIN, D), BF16)

    valid = lax.broadcasted_iota(I32, (WIN, 256), 1) < WIN
    for g in range(3):
        lanes = slice(128 * g, 128 * g + 128)
        biases = []
        for i in range(4):
            h = 4 * g + i
            biases.append(
                jnp.concatenate([bias_ref[h, 0:WIN, :], bias_tail(bias_ref, h, WIN, 18)], axis=1)
            )
        for w in range(2):
            rows = slice(WIN * w, WIN * w + WIN)
            half = upper if w == 0 else lower
            obuf[rows, lanes] = four_heads(
                qbuf[rows, lanes], kpad[w, :, lanes], vpad[w, :, lanes],
                [half(x) for x in biases], valid,
            ).astype(BF16)
    first = (values_ref[...] + dot(obuf[...], wo_ref[...])).astype(BF16)
    first_ref[...] = first
    again = layer_norm(first.astype(F32), gain2_ref[...])
    parts = dot(quadrants_from_natural(), again).astype(BF16)
    for a in range(2):
        west_ref[a] = parts[72 * a : 72 * a + 72]
        east_ref[a] = parts[144 + 72 * a : 144 + 72 * a + 72]


def bias_kernel(
    idx_ref, table_ref, before_ref, lat_ref,
    bias_ref,
    packed, high_ref, low_ref,
):
    pack_table(table_ref, packed.at[1])
    pack_table(before_ref, packed.at[0])

    @pl.when(lat_ref[0] == 0)
    def _():
        packed[0] = packed[1]

    high, low = split_index(idx_ref[...])
    picks, gather_rows = query_picks(), tail_rows(10)
    for a in range(2):
        columns = [key_columns(a, b) for b in range(2)]
        for part, dst in ((high, high_ref), (low, low_ref)):
            rows = dot(picks[80 * a : 80 * a + 80], part).astype(BF16)
            spread = jnp.concatenate(
                [dot(rows[40 * b : 40 * b + 40], columns[b]) for b in range(2)], axis=0
            )
            start = a * 96
            dst[start : start + 80, :] = spread[:, :128].astype(I32)
            tail = fold_tail(spread[:, 128:], gather_rows, 10)
            dst[start + 80 : start + 96, :] = tail.astype(I32)
    for a in range(2):
        expand(packed.at[a], high_ref, low_ref, bias_ref, a * 96, 12)


def second_kernel(
    edge_ref,
    first_ref, west_ref, east_ref, from_west_ref, from_east_ref, north_ref, south_ref,
    wqkv_ref, wo_ref, bias_ref,
    out_ref,
    cat, window, qbuf, kpad, vpad, obuf,
):
    own = (west_ref, east_ref)
    beside = (from_west_ref, from_east_ref)
    beyond = (north_ref, south_ref)
    tokens = jnp.concatenate([west_ref[0], west_ref[1], east_ref[0], east_ref[1]], axis=0)
    asked = dot(queries_from_quadrants(), tokens).astype(BF16)
    qbuf[...] = dot(asked, wqkv_ref[:, 0:D]).astype(BF16).astype(F32)

    order = keys_from_pieces()
    for piece in range(4):
        cat[80 * piece + 72 : 80 * piece + 80, :] = jnp.zeros((8, D), F32)
    for a in range(2):
        for b in range(2):
            q = 2 * a + b
            far = ((1, 0), (2, 3))[b]
            cat[0:72, :] = own[b][a].astype(F32)
            cat[80:152, :] = beside[b][a].astype(F32)
            cat[160:232, :] = beyond[a][far[0]].astype(F32)
            cat[240:312, :] = beyond[a][far[1]].astype(F32)
            window[288 * q : 288 * q + 288, :] = dot(order, cat[...].astype(BF16)).astype(BF16)
    for dst, start in ((kpad, D), (vpad, 2 * D)):
        made = dot(window[...], wqkv_ref[:, start : start + D]).astype(BF16)
        for j in range(8):
            dst[j, 0:WIN, :] = made[WIN * j : WIN * j + WIN]
            dst[j, WIN:, :] = jnp.zeros((256 - WIN, D), BF16)

    shape = (40, 256)
    lane = lax.broadcasted_iota(I32, shape, 1)
    side_q = jnp.minimum(lax.broadcasted_iota(I32, shape, 0) // 18, 1)
    side_k = (lane % 36) // 18
    inside = lane < WIN
    near = lane < 72
    split = side_q == side_k
    for a in range(2):
        open_side = edge_ref[a] > 0
        seen = jnp.logical_and(inside, jnp.logical_or(near, open_side))
        masks = (seen, jnp.logical_and(seen, split))
        for g in range(3):
            lanes = slice(128 * g, 128 * g + 128)
            biases = []
            for i in range(4):
                h = 4 * g + i
                tail = bias_tail(bias_ref, h, 96 * a + 80, 10)
                biases.append(
                    jnp.concatenate([bias_ref[h, 96 * a : 96 * a + 80, :], tail], axis=1)
                )
            for b in range(2):
                for w in range(2):
                    at = 4 * a + 2 * b + w
                    half = upper if w == 0 else lower
                    obuf[40 * at : 40 * at + 40, lanes] = four_heads(
                        qbuf[40 * at : 40 * at + 40, lanes], kpad[at, :, lanes], vpad[at, :, lanes],
                        [half(x[40 * b : 40 * b + 40]) for x in biases], masks[w],
                    )
    attended = dot(given_from_queries(), obuf[...].astype(BF16)).astype(BF16)
    qbuf[0:288, :] = dot(given_from_natural(), first_ref[...]) + dot(attended, wo_ref[...])
    for g in range(72):
        out_ref[g] = qbuf[4 * g : 4 * g + 4, :].astype(BF16)


VMEM = pl.BlockSpec(memory_space=pltpu.VMEM)
SMEM = pl.BlockSpec(memory_space=pltpu.SMEM)
LIMIT = 48 * 1024 * 1024


def shift(block, axis, by, wrap):
    size = lax.axis_size(axis)
    route = [(i, (i + by) % size) for i in range(size) if wrap or 0 <= i + by < size]
    return lax.ppermute(block, axis, route)


def cost(flops, moved):
    return pl.CostEstimate(flops=flops, bytes_accessed=moved, transcendentals=10**6)


def shards(
    tokens, position_index, gain_first, qkv_first, proj_first, bias_first,
    gain_second, qkv_second, proj_second, bias_second,
):
    lat = lax.axis_index("lat")
    last = lax.axis_size("lat") - 1
    params = pltpu.CompilerParams(vmem_limit_bytes=LIMIT)

    first, west, east = pl.pallas_call(
        first_kernel,
        out_shape=(
            jax.ShapeDtypeStruct((288, D), BF16),
            jax.ShapeDtypeStruct((2, 72, D), BF16),
            jax.ShapeDtypeStruct((2, 72, D), BF16),
        ),
        in_specs=[VMEM] * 7,
        out_specs=(VMEM,) * 3,
        scratch_shapes=[
            pltpu.VMEM((288, D), F32),
            pltpu.VMEM((HEADS, CHUNKS * 128), I32),
            pltpu.VMEM((168, 128), I32),
            pltpu.VMEM((168, 128), I32),
            pltpu.VMEM((HEADS, 168, 128), I32),
            pltpu.VMEM((288, D), F32),
            pltpu.VMEM((2, 256, D), BF16),
            pltpu.VMEM((2, 256, D), BF16),
            pltpu.VMEM((288, D), BF16),
        ],
        compiler_params=params,
        cost_estimate=cost(10**9, 3 * 10**6),
        name="first_block",
    )(
        tokens.transpose(1, 2, 0, 3).reshape(72, 4, D), position_index, gain_first, qkv_first, proj_first,
        bias_first.transpose(0, 2, 1, 3).reshape(HEADS, 2, POS), gain_second,
    )

    table = bias_second.transpose(0, 2, 1, 3).reshape(HEADS, 2, POS)
    table, first = lax.optimization_barrier((table, first))
    before = shift(table, "lat", 1, False)
    from_west = shift(east, "lon", 1, True)
    from_east = shift(west, "lon", -1, True)

    bias = pl.pallas_call(
        bias_kernel,
        out_shape=jax.ShapeDtypeStruct((HEADS, 192, 128), I32),
        in_specs=[VMEM] * 3 + [SMEM],
        out_specs=VMEM,
        scratch_shapes=[
            pltpu.VMEM((2, HEADS, CHUNKS * 128), I32),
            pltpu.VMEM((192, 128), I32),
            pltpu.VMEM((192, 128), I32),
        ],
        compiler_params=params,
        cost_estimate=cost(10**9, 10**7),
        name="second_bias",
    )(position_index, table, before, lat.astype(I32).reshape(1))

    west, east, from_west, from_east, bias = lax.optimization_barrier(
        (west, east, from_west, from_east, bias)
    )
    up = jnp.stack([from_west[0], west[0], east[0], from_east[0]])
    down = jnp.stack([from_west[1], west[1], east[1], from_east[1]])
    south = shift(up, "lat", -1, False)
    north = shift(down, "lat", 1, False)

    edges = jnp.stack([lat > 0, lat < last]).astype(I32)
    out = pl.pallas_call(
        second_kernel,
        out_shape=jax.ShapeDtypeStruct((72, 4, D), BF16),
        in_specs=[SMEM] + [VMEM] * 10,
        out_specs=VMEM,
        scratch_shapes=[
            pltpu.VMEM((320, D), F32),
            pltpu.VMEM((1152, D), BF16),
            pltpu.VMEM((320, D), F32),
            pltpu.VMEM((8, 256, D), BF16),
            pltpu.VMEM((8, 256, D), BF16),
            pltpu.VMEM((320, D), F32),
        ],
        compiler_params=params,
        cost_estimate=cost(10**9, 5 * 10**6),
        name="second_block",
    )(
        edges, first, west, east, from_west, from_east, north, south,
        qkv_second, proj_second, bias,
    )
    return out.reshape(6, 12, 4, D).transpose(2, 0, 1, 3)


def solution(mesh):
    return jax.shard_map(
        shards,
        mesh=mesh,
        in_specs=(
            P(None, "lat", "lon", None), P(), P(), P(), P(),
            P("lat", None, None, None), P(), P(), P(), P("lat", None, None, None),
        ),
        out_specs=P(None, "lat", "lon", None),
        check_vma=False,
    )
```

```python
import jax
import jax.numpy as jnp
import numpy as np
from jax import lax
from jax.experimental import pallas as pl
from jax.experimental.pallas import tpu as pltpu
from jax.sharding import PartitionSpec as P

F32, BF16, I32 = jnp.float32, jnp.bfloat16, jnp.int32
HEADS = 12
D = 384
WIN = 144
CHUNKS = 26
POS = 3312
LOG2E = float(np.log2(np.e))
FIX = 8191.0
SCALE = LOG2E * 32 ** -0.5
UNFIX = LOG2E / FIX


def dot(a, b):
    return jnp.dot(a, b, preferred_element_type=F32)


def dot_t(a, b):
    return lax.dot_general(a, b, (((1,), (1,)), ((), ())), preferred_element_type=F32)


def one_hot(source, width):
    lane = lax.broadcasted_iota(I32, (source.shape[0], width), 1)
    return jnp.where(lane == source, 1.0, 0.0).astype(BF16)


def row_ids(count):
    return lax.broadcasted_iota(I32, (count, 1), 0)


def quadrants_from_natural():
    i = row_ids(288)
    b, a, w, lo = i // 144, i // 72 % 2, i // 36 % 2, i // 18 % 2
    level = (2 * w + lo + 1) % 4
    return one_hot(level * 72 + (3 * a + i // 6 % 3) * 12 + 6 * b + i % 6, 288)


def keys_from_pieces():
    i = row_ids(288)
    w, piece, t = i // 144, i // 36 % 4, i % 36
    return one_hot(80 * piece + 36 * w + t, 320)


def queries_from_quadrants():
    i = row_ids(320)
    a, b, w, t = i // 160, i // 80 % 2, i // 40 % 2, i % 40
    return one_hot(jnp.where(t < 36, b * 144 + a * 72 + w * 36 + t, -1), 288)


def natural_from_given():
    i = row_ids(288)
    return one_hot(i % 72 * 4 + i // 72, 288)


def given_from_natural():
    i = row_ids(288)
    return one_hot(i % 4 * 72 + i // 4, 288)


def given_from_queries():
    i = row_ids(288)
    level, r, c = (i % 4 + 3) % 4, i // 48, i // 4 % 12
    a, b, w, lo = r // 3, c // 6, level // 2, level % 2
    return one_hot(a * 160 + b * 80 + w * 40 + lo * 18 + r % 3 * 6 + c % 6, 320)


def tail_rows(tiles):
    packed = -(-tiles // 8) * 8
    shape = (packed, tiles * 8)
    i = lax.broadcasted_iota(I32, shape, 0)
    k = lax.broadcasted_iota(I32, shape, 1)
    take = jnp.logical_and(i // 8 == k // 64, i % 8 == k % 8)
    return jnp.where(take, 1.0, 0.0).astype(BF16)


def tail_columns():
    shape = (WIN, 256)
    i = lax.broadcasted_iota(I32, shape, 0)
    k = lax.broadcasted_iota(I32, shape, 1)
    return jnp.where(i == jnp.where(k < 128, k, 128 + k % 16), 1.0, 0.0).astype(BF16)


def shifted_query(a, b, i):
    return 72 * (i // 18) + 12 * (3 * (1 - a) + i // 6 % 3) + 6 * (1 - b) + i % 6


def shifted_key(a, b, i):
    piece, t = i // 36, i % 36
    row = jnp.where(piece < 2, 3 * (1 - a), 3 * a)
    col = jnp.where(piece % 2 == 0, 6 * (1 - b), 6 * b)
    return 72 * (t // 18) + 12 * (row + t // 6 % 3) + col + t % 6


def query_picks():
    i = row_ids(160)
    a, b, t = i // 80, i // 40 % 2, i % 40
    return one_hot(jnp.where(t < 36, shifted_query(a, b, t), -1), WIN)


def key_columns(a, b):
    k = lax.broadcasted_iota(I32, (1, 256), 1)
    position = shifted_key(a, b, jnp.where(k < 128, k, 128 + k % 16))
    i = lax.broadcasted_iota(I32, (WIN, 256), 0)
    return jnp.where(i == position, 1.0, 0.0).astype(BF16)


def pack_table(table_ref, packed_ref):
    for h in range(HEADS):
        fixed = jnp.round(table_ref[h].astype(F32) * FIX).astype(I32)
        packed_ref[h : h + 1, 0:POS] = (fixed[0:1] << 16) | (fixed[1:2] & 0xFFFF)


def split_index(position_index):
    high = (position_index >> 7).astype(F32).astype(BF16)
    low = (position_index & 127).astype(F32).astype(BF16)
    return high, low


def fold_tail(values, gather_rows, tiles):
    row = lax.broadcasted_iota(I32, values.shape, 0) // 8
    lane = lax.broadcasted_iota(I32, values.shape, 1) // 16
    kept = jnp.where((row % 8) == lane, values, 0.0).astype(BF16)
    return dot(gather_rows, kept)


def place_index(part, columns, gather_rows, dst_ref, start, tiles):
    spread = dot(part, columns)
    rows = tiles * 8
    dst_ref[start : start + rows, :] = spread[:, :128].astype(I32)
    tail = fold_tail(spread[:, 128:], gather_rows, tiles)
    dst_ref[start + rows : start + rows + tail.shape[0], :] = tail.astype(I32)


def expand(packed_ref, high_ref, low_ref, out_ref, start, count):
    def tile(t, carry):
        rows = pl.ds(pl.multiple_of(start + t * 8, 8), 8)
        low = low_ref[rows, :]
        high = high_ref[rows, :]
        picked = [None] * HEADS
        for c in range(CHUNKS):
            here = high == c
            for h in range(HEADS):
                entries = jnp.broadcast_to(packed_ref[h : h + 1, 128 * c : 128 * c + 128], (8, 128))
                got = jnp.take_along_axis(entries, low, axis=1, mode="promise_in_bounds")
                picked[h] = got if c == 0 else jnp.where(here, got, picked[h])
        for h in range(HEADS):
            out_ref[h, rows, :] = picked[h]
        return carry

    lax.fori_loop(0, count, tile, 0)


def bias_tail(bias_ref, h, base, tiles):
    out = []
    for t in range(tiles):
        at = base + (t // 8) * 8
        part = bias_ref[h, at : at + 8, :]
        j = t % 8
        out.append(part if j == 0 else pltpu.roll(part, 128 - 16 * j, 1))
    return jnp.concatenate(out, axis=0)


def upper(packed):
    return (packed >> 16).astype(F32)


def lower(packed):
    return ((packed << 16) >> 16).astype(F32)


def layer_norm(values, gain):
    center = jnp.mean(values, axis=-1, keepdims=True)
    moved = values - center
    spread = jnp.mean(moved * moved, axis=-1, keepdims=True)
    return (moved * lax.rsqrt(spread + 1e-05) * gain).astype(BF16)


def softmax(scores, mask):
    raised = jnp.where(mask, jnp.exp2(scores), 0.0)
    total = jnp.sum(raised, axis=-1, keepdims=True)
    step = jnp.where(total > 1.0, 0.25, 1.0)
    return ((raised * step) * (1.0 / (total * step))).astype(BF16)


def four_heads(query, key, value, biases, mask):
    n = query.shape[0]
    own = lax.broadcasted_iota(I32, query.shape, 1) // 32
    stacked = jnp.concatenate([jnp.where(own == i, query, 0.0) for i in range(4)], axis=0)
    scores = dot_t(stacked.astype(BF16), key)
    probs = [
        softmax(scores[n * i : n * i + n] * SCALE + biases[i] * UNFIX, mask) for i in range(4)
    ]
    parts = dot(jnp.concatenate(probs, axis=0), value)
    out = parts[0:n]
    for i in range(1, 4):
        out = jnp.where(own == i, parts[n * i : n * i + n], out)
    return out


def first_kernel(
    idx_in, table_in, tok_in, wqkv_in, wo_in, gain_in, gain2_in,
    first_ref, west_ref, east_ref,
    idx_ref, table_ref, tok_ref, wqkv_ref, wo_ref, gain_ref, gain2_ref, sems,
    values_ref, packed, high_ref, low_ref, bias_ref, qbuf, kpad, vpad, obuf,
):
    pairs = (
        (idx_in, idx_ref), (table_in, table_ref), (tok_in, tok_ref), (wqkv_in, wqkv_ref),
        (wo_in, wo_ref), (gain_in, gain_ref), (gain2_in, gain2_ref),
    )
    copies = [pltpu.make_async_copy(src, dst, sems.at[i]) for i, (src, dst) in enumerate(pairs)]
    for copy in copies:
        copy.start()
    copies[0].wait()
    copies[1].wait()
    pack_table(table_ref, packed)
    high, low = split_index(idx_ref[...])
    columns, gather_rows = tail_columns(), tail_rows(18)
    place_index(high, columns, gather_rows, high_ref, 0, 18)
    place_index(low, columns, gather_rows, low_ref, 0, 18)
    expand(packed, high_ref, low_ref, bias_ref, 0, 21)

    for copy in copies[2:]:
        copy.wait()
    for g in range(72):
        values_ref[4 * g : 4 * g + 4, :] = tok_ref[g].astype(F32)
    values = dot(natural_from_given(), values_ref[...].astype(BF16))
    values_ref[...] = values
    normed = layer_norm(values, gain_ref[...])
    qkv = dot(normed, wqkv_ref[...]).astype(BF16)
    qbuf[...] = qkv[:, 0:D].astype(F32)
    for w in range(2):
        rows = slice(WIN * w, WIN * w + WIN)
        kpad[w, 0:WIN, :] = qkv[rows, D : 2 * D]
        vpad[w, 0:WIN, :] = qkv[rows, 2 * D :]
        kpad[w, WIN:, :] = jnp.zeros((256 - WIN, D), BF16)
        vpad[w, WIN:, :] = jnp.zeros((256 - WIN, D), BF16)

    valid = lax.broadcasted_iota(I32, (WIN, 256), 1) < WIN
    for g in range(3):
        lanes = slice(128 * g, 128 * g + 128)
        biases = []
        for i in range(4):
            h = 4 * g + i
            biases.append(
                jnp.concatenate([bias_ref[h, 0:WIN, :], bias_tail(bias_ref, h, WIN, 18)], axis=1)
            )
        for w in range(2):
            rows = slice(WIN * w, WIN * w + WIN)
            half = upper if w == 0 else lower
            obuf[rows, lanes] = four_heads(
                qbuf[rows, lanes], kpad[w, :, lanes], vpad[w, :, lanes],
                [half(x) for x in biases], valid,
            ).astype(BF16)
    first = (values_ref[...] + dot(obuf[...], wo_ref[...])).astype(BF16)
    first_ref[...] = first
    again = layer_norm(first.astype(F32), gain2_ref[...])
    parts = dot(quadrants_from_natural(), again).astype(BF16)
    for a in range(2):
        west_ref[a] = parts[72 * a : 72 * a + 72]
        east_ref[a] = parts[144 + 72 * a : 144 + 72 * a + 72]


def fill_bias(lat_ref, idx_in, table_in, before_in, bias_ref, idx_ref, tables, packed, high_ref, low_ref, sems):
    copies = [
        pltpu.make_async_copy(src, dst, sems.at[i])
        for i, (src, dst) in enumerate(
            ((idx_in, idx_ref), (before_in, tables.at[0]), (table_in, tables.at[1]))
        )
    ]
    for copy in copies:
        copy.start()
    for copy in copies:
        copy.wait()
    pack_table(tables.at[0], packed.at[0])
    pack_table(tables.at[1], packed.at[1])

    @pl.when(lat_ref[0] == 0)
    def _():
        packed[0] = packed[1]

    high, low = split_index(idx_ref[...])
    picks, gather_rows = query_picks(), tail_rows(10)
    for a in range(2):
        columns = [key_columns(a, b) for b in range(2)]
        for part, dst in ((high, high_ref), (low, low_ref)):
            rows = dot(picks[80 * a : 80 * a + 80], part).astype(BF16)
            spread = jnp.concatenate(
                [dot(rows[40 * b : 40 * b + 40], columns[b]) for b in range(2)], axis=0
            )
            start = a * 96
            dst[start : start + 80, :] = spread[:, :128].astype(I32)
            tail = fold_tail(spread[:, 128:], gather_rows, 10)
            dst[start + 80 : start + 96, :] = tail.astype(I32)
    for a in range(2):
        expand(packed.at[a], high_ref, low_ref, bias_ref, a * 96, 12)


def early_kernel(where_ref, idx_in, table_in, before_in, bias_ref, *scratch):
    @pl.when(where_ref[1] == 1)
    def _():
        fill_bias(where_ref, idx_in, table_in, before_in, bias_ref, *scratch)


def late_kernel(where_ref, idx_in, table_in, before_in, bias_in, bias_ref, *scratch):
    @pl.when(where_ref[1] == 0)
    def _():
        fill_bias(where_ref, idx_in, table_in, before_in, bias_ref, *scratch)


def second_kernel(
    edge_ref,
    first_ref, west_ref, east_ref, from_west_ref, from_east_ref, north_ref, south_ref,
    wqkv_ref, wo_ref, bias_ref,
    out_ref,
    cat, window, qbuf, kpad, vpad, obuf,
):
    own = (west_ref, east_ref)
    beside = (from_west_ref, from_east_ref)
    beyond = (north_ref, south_ref)
    tokens = jnp.concatenate([west_ref[0], west_ref[1], east_ref[0], east_ref[1]], axis=0)
    asked = dot(queries_from_quadrants(), tokens).astype(BF16)
    qbuf[...] = dot(asked, wqkv_ref[:, 0:D]).astype(BF16).astype(F32)

    order = keys_from_pieces()
    for piece in range(4):
        cat[80 * piece + 72 : 80 * piece + 80, :] = jnp.zeros((8, D), F32)
    for a in range(2):
        for b in range(2):
            q = 2 * a + b
            far = ((1, 0), (2, 3))[b]
            cat[0:72, :] = own[b][a].astype(F32)
            cat[80:152, :] = beside[b][a].astype(F32)
            cat[160:232, :] = beyond[a][far[0]].astype(F32)
            cat[240:312, :] = beyond[a][far[1]].astype(F32)
            window[288 * q : 288 * q + 288, :] = dot(order, cat[...].astype(BF16)).astype(BF16)
    for dst, start in ((kpad, D), (vpad, 2 * D)):
        made = dot(window[...], wqkv_ref[:, start : start + D]).astype(BF16)
        for j in range(8):
            dst[j, 0:WIN, :] = made[WIN * j : WIN * j + WIN]
            dst[j, WIN:, :] = jnp.zeros((256 - WIN, D), BF16)

    shape = (40, 256)
    lane = lax.broadcasted_iota(I32, shape, 1)
    side_q = jnp.minimum(lax.broadcasted_iota(I32, shape, 0) // 18, 1)
    side_k = (lane % 36) // 18
    inside = lane < WIN
    near = lane < 72
    split = side_q == side_k
    for a in range(2):
        open_side = edge_ref[a] > 0
        seen = jnp.logical_and(inside, jnp.logical_or(near, open_side))
        masks = (seen, jnp.logical_and(seen, split))
        for g in range(3):
            lanes = slice(128 * g, 128 * g + 128)
            biases = []
            for i in range(4):
                h = 4 * g + i
                tail = bias_tail(bias_ref, h, 96 * a + 80, 10)
                biases.append(
                    jnp.concatenate([bias_ref[h, 96 * a : 96 * a + 80, :], tail], axis=1)
                )
            for b in range(2):
                for w in range(2):
                    at = 4 * a + 2 * b + w
                    half = upper if w == 0 else lower
                    obuf[40 * at : 40 * at + 40, lanes] = four_heads(
                        qbuf[40 * at : 40 * at + 40, lanes], kpad[at, :, lanes], vpad[at, :, lanes],
                        [half(x[40 * b : 40 * b + 40]) for x in biases], masks[w],
                    )
    attended = dot(given_from_queries(), obuf[...].astype(BF16)).astype(BF16)
    qbuf[0:288, :] = dot(given_from_natural(), first_ref[...]) + dot(attended, wo_ref[...])
    for g in range(72):
        out_ref[g] = qbuf[4 * g : 4 * g + 4, :].astype(BF16)


VMEM = pl.BlockSpec(memory_space=pltpu.VMEM)
SMEM = pl.BlockSpec(memory_space=pltpu.SMEM)
HBM = pl.BlockSpec(memory_space=pltpu.HBM)
ANY = pl.BlockSpec(memory_space=pl.ANY)
LIMIT = 32 * 1024 * 1024
WIDE = 60 * 1024 * 1024


def shift(block, axis, by, wrap):
    size = lax.axis_size(axis)
    route = [(i, (i + by) % size) for i in range(size) if wrap or 0 <= i + by < size]
    return lax.ppermute(block, axis, route)


def cost(flops, moved):
    return pl.CostEstimate(flops=flops, bytes_accessed=moved, transcendentals=10**6)


def shards(
    tokens, position_index, gain_first, qkv_first, proj_first, bias_first,
    gain_second, qkv_second, proj_second, bias_second,
):
    lat = lax.axis_index("lat")
    last = lax.axis_size("lat") - 1
    params = pltpu.CompilerParams(vmem_limit_bytes=LIMIT)

    part = max(1, lax.axis_size("lon") // 2)
    where = jnp.stack([lat, (lax.axis_index("lon") % part == 0).astype(lat.dtype)]).astype(I32)
    table = bias_second.transpose(0, 2, 1, 3).reshape(HEADS, 2, POS)
    before = shift(table, "lat", 1, False)

    first, west, east = pl.pallas_call(
        first_kernel,
        out_shape=(
            jax.ShapeDtypeStruct((288, D), BF16),
            jax.ShapeDtypeStruct((2, 72, D), BF16),
            jax.ShapeDtypeStruct((2, 72, D), BF16),
        ),
        in_specs=[HBM] * 7,
        out_specs=(VMEM,) * 3,
        scratch_shapes=[
            pltpu.VMEM((WIN, WIN), I32),
            pltpu.VMEM((HEADS, 2, POS), BF16),
            pltpu.VMEM((72, 4, D), BF16),
            pltpu.VMEM((D, 3 * D), BF16),
            pltpu.VMEM((D, D), BF16),
            pltpu.VMEM((D,), F32),
            pltpu.VMEM((D,), F32),
            pltpu.SemaphoreType.DMA((7,)),
            pltpu.VMEM((288, D), F32),
            pltpu.VMEM((HEADS, CHUNKS * 128), I32),
            pltpu.VMEM((168, 128), I32),
            pltpu.VMEM((168, 128), I32),
            pltpu.VMEM((HEADS, 168, 128), I32),
            pltpu.VMEM((288, D), F32),
            pltpu.VMEM((2, 256, D), BF16),
            pltpu.VMEM((2, 256, D), BF16),
            pltpu.VMEM((288, D), BF16),
        ],
        compiler_params=pltpu.CompilerParams(vmem_limit_bytes=WIDE),
        cost_estimate=cost(10**9, 3 * 10**6),
        name="first_block",
    )(
        position_index,
        bias_first.transpose(0, 2, 1, 3).reshape(HEADS, 2, POS),
        tokens.transpose(1, 2, 0, 3).reshape(72, 4, D),
        qkv_first, proj_first, gain_first, gain_second,
    )

    bias_shape = jax.ShapeDtypeStruct((HEADS, 192, 128), I32)
    bias_scratch = [
        pltpu.VMEM((WIN, WIN), I32),
        pltpu.VMEM((2, HEADS, 2, POS), BF16),
        pltpu.VMEM((2, HEADS, CHUNKS * 128), I32),
        pltpu.VMEM((192, 128), I32),
        pltpu.VMEM((192, 128), I32),
        pltpu.SemaphoreType.DMA((3,)),
    ]
    before, west, east = lax.optimization_barrier((before, west, east))
    bias = pl.pallas_call(
        early_kernel,
        out_shape=bias_shape,
        in_specs=[SMEM, HBM, HBM, ANY],
        out_specs=VMEM,
        scratch_shapes=bias_scratch,
        compiler_params=params,
        cost_estimate=cost(10**6, 10**5),
        name="early_bias",
    )(where, position_index, table, before)
    bias, west, east = lax.optimization_barrier((bias, west, east))
    from_east = shift(west, "lon", -1, True)
    from_west = shift(east, "lon", 1, True)
    bias = pl.pallas_call(
        late_kernel,
        out_shape=bias_shape,
        in_specs=[SMEM, HBM, HBM, ANY, VMEM],
        out_specs=VMEM,
        scratch_shapes=bias_scratch,
        input_output_aliases={4: 0},
        compiler_params=params,
        cost_estimate=cost(10**9, 10**7),
        name="late_bias",
    )(where, position_index, table, before, bias)

    west, east, from_west, from_east, bias = lax.optimization_barrier(
        (west, east, from_west, from_east, bias)
    )
    up = jnp.stack([from_west[0], west[0], east[0], from_east[0]])
    down = jnp.stack([from_west[1], west[1], east[1], from_east[1]])
    south = shift(up, "lat", -1, False)
    north = shift(down, "lat", 1, False)

    edges = jnp.stack([lat > 0, lat < last]).astype(I32)
    out = pl.pallas_call(
        second_kernel,
        out_shape=jax.ShapeDtypeStruct((72, 4, D), BF16),
        in_specs=[SMEM] + [VMEM] * 10,
        out_specs=VMEM,
        scratch_shapes=[
            pltpu.VMEM((320, D), F32),
            pltpu.VMEM((1152, D), BF16),
            pltpu.VMEM((320, D), F32),
            pltpu.VMEM((8, 256, D), BF16),
            pltpu.VMEM((8, 256, D), BF16),
            pltpu.VMEM((320, D), F32),
        ],
        compiler_params=params,
        cost_estimate=cost(10**9, 5 * 10**6),
        name="second_block",
    )(
        edges, first, west, east, from_west, from_east, north, south,
        qkv_second, proj_second, bias,
    )
    return out.reshape(6, 12, 4, D).transpose(2, 0, 1, 3)


def solution(mesh):
    return jax.shard_map(
        shards,
        mesh=mesh,
        in_specs=(
            P(None, "lat", "lon", None), P(), P(), P(), P(),
            P("lat", None, None, None), P(), P(), P(), P("lat", None, None, None),
        ),
        out_specs=P(None, "lat", "lon", None),
        check_vma=False,
    )
```

```python
import jax
import jax.numpy as jnp
import numpy as np
from jax import lax
from jax.experimental import pallas as pl
from jax.experimental.pallas import tpu as pltpu
from jax.sharding import PartitionSpec as P

F32, BF16, I32 = jnp.float32, jnp.bfloat16, jnp.int32
HEADS = 12
D = 384
WIN = 144
CHUNKS = 26
POS = 3312
LOG2E = float(np.log2(np.e))
FIELDS = ((11, 256.0, 21), (11, 256.0, 10), (10, 128.0, 0))
SCALE = LOG2E * 32 ** -0.5


def dot(a, b):
    return jnp.dot(a, b, preferred_element_type=F32)


def dot_t(a, b):
    return lax.dot_general(a, b, (((1,), (1,)), ((), ())), preferred_element_type=F32)


def one_hot(source, width):
    lane = lax.broadcasted_iota(I32, (source.shape[0], width), 1)
    return jnp.where(lane == source, 1.0, 0.0).astype(BF16)


def row_ids(count):
    return lax.broadcasted_iota(I32, (count, 1), 0)


def quadrants_from_natural():
    i = row_ids(288)
    b, a, w, lo = i // 144, i // 72 % 2, i // 36 % 2, i // 18 % 2
    level = (2 * w + lo + 1) % 4
    return one_hot(level * 72 + (3 * a + i // 6 % 3) * 12 + 6 * b + i % 6, 288)


def keys_from_pieces():
    i = row_ids(288)
    w, piece, t = i // 144, i // 36 % 4, i % 36
    return one_hot(80 * piece + 36 * w + t, 320)


def queries_from_quadrants():
    i = row_ids(320)
    a, b, w, t = i // 160, i // 80 % 2, i // 40 % 2, i % 40
    return one_hot(jnp.where(t < 36, b * 144 + a * 72 + w * 36 + t, -1), 288)


def natural_from_given():
    i = row_ids(288)
    return one_hot(i % 72 * 4 + i // 72, 288)


def given_from_natural():
    i = row_ids(288)
    return one_hot(i % 4 * 72 + i // 4, 288)


def given_from_queries():
    i = row_ids(288)
    level, r, c = (i % 4 + 3) % 4, i // 48, i // 4 % 12
    a, b, w, lo = r // 3, c // 6, level // 2, level % 2
    return one_hot(a * 160 + b * 80 + w * 40 + lo * 18 + r % 3 * 6 + c % 6, 320)


def tail_rows(tiles):
    packed = -(-tiles // 8) * 8
    shape = (packed, tiles * 8)
    i = lax.broadcasted_iota(I32, shape, 0)
    k = lax.broadcasted_iota(I32, shape, 1)
    take = jnp.logical_and(i // 8 == k // 64, i % 8 == k % 8)
    return jnp.where(take, 1.0, 0.0).astype(BF16)


def tail_columns():
    shape = (WIN, 256)
    i = lax.broadcasted_iota(I32, shape, 0)
    k = lax.broadcasted_iota(I32, shape, 1)
    return jnp.where(i == jnp.where(k < 128, k, 128 + k % 16), 1.0, 0.0).astype(BF16)


def shifted_query(a, b, i):
    return 72 * (i // 18) + 12 * (3 * (1 - a) + i // 6 % 3) + 6 * (1 - b) + i % 6


def shifted_key(a, b, i):
    piece, t = i // 36, i % 36
    row = jnp.where(piece < 2, 3 * (1 - a), 3 * a)
    col = jnp.where(piece % 2 == 0, 6 * (1 - b), 6 * b)
    return 72 * (t // 18) + 12 * (row + t // 6 % 3) + col + t % 6


def query_picks():
    i = row_ids(160)
    a, b, t = i // 80, i // 40 % 2, i % 40
    return one_hot(jnp.where(t < 36, shifted_query(a, b, t), -1), WIN)


def key_columns(a, b):
    k = lax.broadcasted_iota(I32, (1, 256), 1)
    position = shifted_key(a, b, jnp.where(k < 128, k, 128 + k % 16))
    i = lax.broadcasted_iota(I32, (WIN, 256), 0)
    return jnp.where(i == position, 1.0, 0.0).astype(BF16)


def pack_table(table_ref, packed_ref):
    for i in range(4):
        word = None
        for g, (bits, steps, place) in enumerate(FIELDS):
            top = 2.0 ** (bits - 1) - 1
            fixed = jnp.minimum(jnp.round(table_ref[4 * g + i].astype(F32) * steps), top).astype(I32)
            field = (fixed & (2**bits - 1)) << place
            word = field if word is None else word | field
        packed_ref[2 * i : 2 * i + 2, 0:POS] = word


def unpack(words, g):
    bits, steps, place = FIELDS[g]
    fixed = (words << (32 - bits - place)) >> (32 - bits)
    return fixed.astype(F32) * (LOG2E / steps)


def split_index(position_index):
    high = (position_index >> 7).astype(F32).astype(BF16)
    low = (position_index & 127).astype(F32).astype(BF16)
    return high, low


def fold_tail(values, gather_rows, tiles):
    row = lax.broadcasted_iota(I32, values.shape, 0) // 8
    lane = lax.broadcasted_iota(I32, values.shape, 1) // 16
    kept = jnp.where((row % 8) == lane, values, 0.0).astype(BF16)
    return dot(gather_rows, kept)


def place_index(part, columns, gather_rows, dst_ref, start, tiles):
    spread = dot(part, columns)
    rows = tiles * 8
    dst_ref[start : start + rows, :] = spread[:, :128].astype(I32)
    tail = fold_tail(spread[:, 128:], gather_rows, tiles)
    dst_ref[start + rows : start + rows + tail.shape[0], :] = tail.astype(I32)


def expand(packed_ref, high_ref, low_ref, main_ref, tail_ref, tiles):
    def picked(t):
        rows = pl.ds(pl.multiple_of(t * 8, 8), 8)
        low = low_ref[rows, :]
        high = high_ref[rows, :]
        words = [None] * 8
        for c in range(CHUNKS):
            here = high == c
            for r in range(8):
                entries = jnp.broadcast_to(packed_ref[r : r + 1, 128 * c : 128 * c + 128], (8, 128))
                got = jnp.take_along_axis(entries, low, axis=1, mode="promise_in_bounds")
                words[r] = got if c == 0 else jnp.where(here, got, words[r])
        return words

    def main(t, carry):
        for r, words in enumerate(picked(t)):
            main_ref[r, pl.ds(pl.multiple_of(t * 8, 8), 8), :] = words
        return carry

    def tail(v, carry):
        for r, words in enumerate(picked(tiles + v)):
            tail_ref[r, pl.ds(pl.multiple_of(v * 64, 64), 8), :] = words
            for j in range(1, 8):
                at = pl.multiple_of(v * 64 + 8 * j, 8)
                tail_ref[r, pl.ds(at, 8), :] = pltpu.roll(words, 128 - 16 * j, 1)
        return carry

    lax.fori_loop(0, tiles, main, 0)
    lax.fori_loop(0, -(-tiles // 8), tail, 0)


def layer_norm(values, gain):
    center = jnp.mean(values, axis=-1, keepdims=True)
    moved = values - center
    spread = jnp.mean(moved * moved, axis=-1, keepdims=True)
    return (moved * lax.rsqrt(spread + 1e-05) * gain).astype(BF16)


def softmax(scores, mask):
    raised = jnp.where(mask, jnp.exp2(scores), 0.0)
    total = jnp.sum(raised, axis=-1, keepdims=True)
    step = jnp.where(total > 1.0, 0.25, 1.0)
    return ((raised * step) * (1.0 / (total * step))).astype(BF16)


def four_heads(query, key, value, biases, mask):
    n = query.shape[0]
    own = lax.broadcasted_iota(I32, query.shape, 1) // 32
    stacked = jnp.concatenate([jnp.where(own == i, query, 0.0) for i in range(4)], axis=0)
    scores = dot_t(stacked.astype(BF16), key)
    probs = [
        softmax(scores[n * i : n * i + n] * SCALE + biases[i], mask) for i in range(4)
    ]
    parts = dot(jnp.concatenate(probs, axis=0), value)
    out = parts[0:n]
    for i in range(1, 4):
        out = jnp.where(own == i, parts[n * i : n * i + n], out)
    return out


def first_kernel(
    idx_in, table_in, tok_in, wqkv_in, wo_in, gain_in, gain2_in,
    first_ref, west_ref, east_ref,
    idx_ref, table_ref, tok_ref, wqkv_ref, wo_ref, gain_ref, gain2_ref, sems,
    values_ref, packed, high_ref, low_ref, main_ref, tail_ref, qbuf, kpad, vpad, obuf,
):
    pairs = (
        (idx_in, idx_ref), (table_in, table_ref), (tok_in, tok_ref), (wqkv_in, wqkv_ref),
        (wo_in, wo_ref), (gain_in, gain_ref), (gain2_in, gain2_ref),
    )
    copies = [pltpu.make_async_copy(src, dst, sems.at[i]) for i, (src, dst) in enumerate(pairs)]
    for copy in copies:
        copy.start()
    copies[0].wait()
    copies[1].wait()
    pack_table(table_ref, packed)
    high, low = split_index(idx_ref[...])
    columns, gather_rows = tail_columns(), tail_rows(18)
    place_index(high, columns, gather_rows, high_ref, 0, 18)
    place_index(low, columns, gather_rows, low_ref, 0, 18)
    expand(packed, high_ref, low_ref, main_ref, tail_ref, 18)

    for copy in copies[2:]:
        copy.wait()
    for g in range(72):
        values_ref[4 * g : 4 * g + 4, :] = tok_ref[g].astype(F32)
    values = dot(natural_from_given(), values_ref[...].astype(BF16))
    values_ref[...] = values
    normed = layer_norm(values, gain_ref[...])
    qkv = dot(normed, wqkv_ref[...]).astype(BF16)
    qbuf[...] = qkv[:, 0:D].astype(F32)
    for w in range(2):
        rows = slice(WIN * w, WIN * w + WIN)
        kpad[w, 0:WIN, :] = qkv[rows, D : 2 * D]
        vpad[w, 0:WIN, :] = qkv[rows, 2 * D :]
        kpad[w, WIN:, :] = jnp.zeros((256 - WIN, D), BF16)
        vpad[w, WIN:, :] = jnp.zeros((256 - WIN, D), BF16)

    valid = lax.broadcasted_iota(I32, (WIN, 256), 1) < WIN
    for g in range(3):
        lanes = slice(128 * g, 128 * g + 128)
        for w in range(2):
            rows = slice(WIN * w, WIN * w + WIN)
            biases = [
                unpack(
                    jnp.concatenate([main_ref[2 * i + w], tail_ref[2 * i + w, 0:WIN, :]], axis=1), g
                )
                for i in range(4)
            ]
            obuf[rows, lanes] = four_heads(
                qbuf[rows, lanes], kpad[w, :, lanes], vpad[w, :, lanes], biases, valid
            ).astype(BF16)
    first = (values_ref[...] + dot(obuf[...], wo_ref[...])).astype(BF16)
    first_ref[...] = first
    again = layer_norm(first.astype(F32), gain2_ref[...])
    parts = dot(quadrants_from_natural(), again).astype(BF16)
    for a in range(2):
        west_ref[a] = parts[72 * a : 72 * a + 72]
        east_ref[a] = parts[144 + 72 * a : 144 + 72 * a + 72]


def fill_bias(
    where_ref, idx_in, table_in, before_in, main_ref, tail_ref,
    idx_ref, tables, packed, high_ref, low_ref, sems,
):
    copies = [
        pltpu.make_async_copy(src, dst, sems.at[i])
        for i, (src, dst) in enumerate(
            ((idx_in, idx_ref), (before_in, tables.at[0]), (table_in, tables.at[1]))
        )
    ]
    for copy in copies:
        copy.start()
    for copy in copies:
        copy.wait()
    pack_table(tables.at[0], packed.at[0])
    pack_table(tables.at[1], packed.at[1])

    @pl.when(where_ref[0] == 0)
    def _():
        packed[0] = packed[1]

    high, low = split_index(idx_ref[...])
    picks, gather_rows = query_picks(), tail_rows(10)
    for a in range(2):
        columns = [key_columns(a, b) for b in range(2)]
        for part, dst in ((high, high_ref), (low, low_ref)):
            rows = dot(picks[80 * a : 80 * a + 80], part).astype(BF16)
            spread = jnp.concatenate(
                [dot(rows[40 * b : 40 * b + 40], columns[b]) for b in range(2)], axis=0
            )
            dst[a, 0:80, :] = spread[:, :128].astype(I32)
            tail = fold_tail(spread[:, 128:], gather_rows, 10)
            dst[a, 80:96, :] = tail.astype(I32)
    for a in range(2):
        expand(packed.at[a], high_ref.at[a], low_ref.at[a], main_ref.at[a], tail_ref.at[a], 10)


def early_kernel(where_ref, idx_in, table_in, before_in, main_ref, tail_ref, *scratch):
    @pl.when(where_ref[1] == 1)
    def _():
        fill_bias(where_ref, idx_in, table_in, before_in, main_ref, tail_ref, *scratch)


def late_kernel(
    where_ref, idx_in, table_in, before_in, main_in, tail_in, main_ref, tail_ref, *scratch
):
    @pl.when(where_ref[1] == 0)
    def _():
        fill_bias(where_ref, idx_in, table_in, before_in, main_ref, tail_ref, *scratch)

    @pl.when(where_ref[1] == 1)
    def _():
        main_ref[...] = main_in[...]
        tail_ref[...] = tail_in[...]


def stack_kernel(where_ref, west_ref, east_ref, from_west_ref, from_east_ref, seam_ref, up_ref, down_ref):
    for a, dst in enumerate((up_ref, down_ref)):
        dst[0] = from_west_ref[a]
        dst[1] = west_ref[a]
        dst[2] = east_ref[a]
        dst[3] = jnp.where(where_ref[2] == 1, seam_ref[a], from_east_ref[a])


def second_kernel(
    edge_ref,
    first_ref, up_ref, down_ref, north_ref, south_ref,
    wqkv_ref, wo_ref, main_ref, tail_ref,
    out_ref,
    cat, window, qbuf, kpad, vpad, obuf,
):
    here = (up_ref, down_ref)
    beyond = (north_ref, south_ref)
    tokens = jnp.concatenate([up_ref[1], down_ref[1], up_ref[2], down_ref[2]], axis=0)
    asked = dot(queries_from_quadrants(), tokens).astype(BF16)
    qbuf[...] = dot(asked, wqkv_ref[:, 0:D]).astype(BF16).astype(F32)

    order = keys_from_pieces()
    for piece in range(4):
        cat[80 * piece + 72 : 80 * piece + 80, :] = jnp.zeros((8, D), F32)
    for a in range(2):
        for b in range(2):
            q = 2 * a + b
            far = ((1, 0), (2, 3))[b]
            cat[0:72, :] = here[a][1 + b].astype(F32)
            cat[80:152, :] = here[a][3 * b].astype(F32)
            cat[160:232, :] = beyond[a][far[0]].astype(F32)
            cat[240:312, :] = beyond[a][far[1]].astype(F32)
            window[288 * q : 288 * q + 288, :] = dot(order, cat[...].astype(BF16)).astype(BF16)
    for dst, start in ((kpad, D), (vpad, 2 * D)):
        made = dot(window[...], wqkv_ref[:, start : start + D]).astype(BF16)
        for j in range(8):
            dst[j, 0:WIN, :] = made[WIN * j : WIN * j + WIN]
            dst[j, WIN:, :] = jnp.zeros((256 - WIN, D), BF16)

    shape = (40, 256)
    lane = lax.broadcasted_iota(I32, shape, 1)
    side_q = jnp.minimum(lax.broadcasted_iota(I32, shape, 0) // 18, 1)
    side_k = (lane % 36) // 18
    inside = lane < WIN
    near = lane < 72
    split = side_q == side_k
    for a in range(2):
        open_side = edge_ref[a] > 0
        seen = jnp.logical_and(inside, jnp.logical_or(near, open_side))
        masks = (seen, jnp.logical_and(seen, split))
        for g in range(3):
            lanes = slice(128 * g, 128 * g + 128)
            for b in range(2):
                rows = slice(40 * b, 40 * b + 40)
                for w in range(2):
                    at = 4 * a + 2 * b + w
                    biases = [
                        unpack(
                            jnp.concatenate(
                                [main_ref[a, 2 * i + w, rows, :], tail_ref[a, 2 * i + w, rows, :]], axis=1
                            ),
                            g,
                        )
                        for i in range(4)
                    ]
                    obuf[40 * at : 40 * at + 40, lanes] = four_heads(
                        qbuf[40 * at : 40 * at + 40, lanes], kpad[at, :, lanes], vpad[at, :, lanes],
                        biases, masks[w],
                    )
    attended = dot(given_from_queries(), obuf[...].astype(BF16)).astype(BF16)
    qbuf[0:288, :] = dot(given_from_natural(), first_ref[...]) + dot(attended, wo_ref[...])
    for g in range(72):
        out_ref[g] = qbuf[4 * g : 4 * g + 4, :].astype(BF16)


VMEM = pl.BlockSpec(memory_space=pltpu.VMEM)
SMEM = pl.BlockSpec(memory_space=pltpu.SMEM)
HBM = pl.BlockSpec(memory_space=pltpu.HBM)
ANY = pl.BlockSpec(memory_space=pl.ANY)
LIMIT = 32 * 1024 * 1024
WIDE = 60 * 1024 * 1024


def shift(block, axis, by, wrap):
    size = lax.axis_size(axis)
    route = [(i, (i + by) % size) for i in range(size) if wrap or 0 <= i + by < size]
    return lax.ppermute(block, axis, route)


def cost(flops, moved):
    return pl.CostEstimate(flops=flops, bytes_accessed=moved, transcendentals=10**6)


def shards(
    tokens, position_index, gain_first, qkv_first, proj_first, bias_first,
    gain_second, qkv_second, proj_second, bias_second,
):
    lat = lax.axis_index("lat")
    last = lax.axis_size("lat") - 1
    params = pltpu.CompilerParams(vmem_limit_bytes=LIMIT)

    part = lax.axis_size("lon") // 2
    place = lax.axis_index("lon") % part
    where = jnp.stack([lat, (place == 0).astype(lat.dtype), (place == part - 1).astype(lat.dtype)])
    where = where.astype(I32)
    table = bias_second.transpose(0, 2, 1, 3).reshape(HEADS, 2, POS)
    before = shift(table, "lat", 1, False)

    first, west, east = pl.pallas_call(
        first_kernel,
        out_shape=(
            jax.ShapeDtypeStruct((288, D), BF16),
            jax.ShapeDtypeStruct((2, 72, D), BF16),
            jax.ShapeDtypeStruct((2, 72, D), BF16),
        ),
        in_specs=[HBM] * 7,
        out_specs=(VMEM,) * 3,
        scratch_shapes=[
            pltpu.VMEM((WIN, WIN), I32),
            pltpu.VMEM((HEADS, 2, POS), BF16),
            pltpu.VMEM((72, 4, D), BF16),
            pltpu.VMEM((D, 3 * D), BF16),
            pltpu.VMEM((D, D), BF16),
            pltpu.VMEM((D,), F32),
            pltpu.VMEM((D,), F32),
            pltpu.SemaphoreType.DMA((7,)),
            pltpu.VMEM((288, D), F32),
            pltpu.VMEM((8, CHUNKS * 128), I32),
            pltpu.VMEM((168, 128), I32),
            pltpu.VMEM((168, 128), I32),
            pltpu.VMEM((8, WIN, 128), I32),
            pltpu.VMEM((8, 192, 128), I32),
            pltpu.VMEM((288, D), F32),
            pltpu.VMEM((2, 256, D), BF16),
            pltpu.VMEM((2, 256, D), BF16),
            pltpu.VMEM((288, D), BF16),
        ],
        compiler_params=pltpu.CompilerParams(vmem_limit_bytes=WIDE),
        cost_estimate=cost(10**9, 3 * 10**6),
        name="first_block",
    )(
        position_index,
        bias_first.transpose(0, 2, 1, 3).reshape(HEADS, 2, POS),
        tokens.transpose(1, 2, 0, 3).reshape(72, 4, D),
        qkv_first, proj_first, gain_first, gain_second,
    )

    bias_shapes = (
        jax.ShapeDtypeStruct((2, 8, 80, 128), I32),
        jax.ShapeDtypeStruct((2, 8, 128, 128), I32),
    )
    bias_scratch = [
        pltpu.VMEM((WIN, WIN), I32),
        pltpu.VMEM((2, HEADS, 2, POS), BF16),
        pltpu.VMEM((2, 8, CHUNKS * 128), I32),
        pltpu.VMEM((2, 96, 128), I32),
        pltpu.VMEM((2, 96, 128), I32),
        pltpu.SemaphoreType.DMA((3,)),
    ]
    from_west = shift(east, "lon", 1, True)
    size = lax.axis_size("lon")
    inner = [(i, i - 1) for i in range(size) if i % part]
    seam = [(i, (i - 1) % size) for i in range(size) if i % part == 0]
    from_east = lax.ppermute(west, "lon", inner)
    before, west = lax.optimization_barrier((before, west))
    main, tail = pl.pallas_call(
        early_kernel,
        out_shape=bias_shapes,
        in_specs=[SMEM, HBM, HBM, ANY],
        out_specs=(VMEM, VMEM),
        scratch_shapes=bias_scratch,
        compiler_params=params,
        cost_estimate=cost(10**6, 10**5),
        name="early_bias",
    )(where, position_index, table, before)
    main, tail, west = lax.optimization_barrier((main, tail, west))
    from_seam = lax.ppermute(west, "lon", seam)
    main, tail = pl.pallas_call(
        late_kernel,
        out_shape=bias_shapes,
        in_specs=[SMEM, HBM, HBM, ANY, VMEM, VMEM],
        out_specs=(VMEM, VMEM),
        scratch_shapes=bias_scratch,
        compiler_params=params,
        cost_estimate=cost(10**9, 10**7),
        name="late_bias",
    )(where, position_index, table, before, main, tail)

    west, east, from_west, from_east, from_seam, main, tail = lax.optimization_barrier(
        (west, east, from_west, from_east, from_seam, main, tail)
    )
    pieces = jax.ShapeDtypeStruct((4, 72, D), BF16)
    up, down = pl.pallas_call(
        stack_kernel,
        out_shape=(pieces, pieces),
        in_specs=[SMEM] + [VMEM] * 5,
        out_specs=(VMEM, VMEM),
        compiler_params=params,
        cost_estimate=cost(10**5, 10**6),
        name="stack_pieces",
    )(where, west, east, from_west, from_east, from_seam)
    south = shift(up, "lat", -1, False)
    north = shift(down, "lat", 1, False)

    edges = jnp.stack([lat > 0, lat < last]).astype(I32)
    out = pl.pallas_call(
        second_kernel,
        out_shape=jax.ShapeDtypeStruct((72, 4, D), BF16),
        in_specs=[SMEM] + [VMEM] * 9,
        out_specs=VMEM,
        scratch_shapes=[
            pltpu.VMEM((320, D), F32),
            pltpu.VMEM((1152, D), BF16),
            pltpu.VMEM((320, D), F32),
            pltpu.VMEM((8, 256, D), BF16),
            pltpu.VMEM((8, 256, D), BF16),
            pltpu.VMEM((320, D), F32),
        ],
        compiler_params=params,
        cost_estimate=cost(10**9, 5 * 10**6),
        name="second_block",
    )(
        edges, first, up, down, north, south, qkv_second, proj_second, main, tail,
    )
    return out.reshape(6, 12, 4, D).transpose(2, 0, 1, 3)


def solution(mesh):
    return jax.shard_map(
        shards,
        mesh=mesh,
        in_specs=(
            P(None, "lat", "lon", None), P(), P(), P(), P(),
            P("lat", None, None, None), P(), P(), P(), P("lat", None, None, None),
        ),
        out_specs=P(None, "lat", "lon", None),
        check_vma=False,
    )
```

```python
import jax
import jax.numpy as jnp
import numpy as np
from jax import lax
from jax.experimental import pallas as pl
from jax.experimental.pallas import tpu as pltpu
from jax.sharding import PartitionSpec as P

F32, BF16, I32 = jnp.float32, jnp.bfloat16, jnp.int32
HEADS = 12
D = 384
WIN = 144
CHUNKS = 26
POS = 3312
LOG2E = float(np.log2(np.e))
FIELDS = ((11, 256.0, 21), (11, 256.0, 10), (10, 128.0, 0))
SCALE = LOG2E * 32 ** -0.5


def dot(a, b):
    return jnp.dot(a, b, preferred_element_type=F32)


def dot_t(a, b):
    return lax.dot_general(a, b, (((1,), (1,)), ((), ())), preferred_element_type=F32)


def one_hot(source, width):
    lane = lax.broadcasted_iota(I32, (source.shape[0], width), 1)
    return jnp.where(lane == source, 1.0, 0.0).astype(BF16)


def row_ids(count):
    return lax.broadcasted_iota(I32, (count, 1), 0)


def quadrants_from_natural():
    i = row_ids(288)
    b, a, w, lo = i // 144, i // 72 % 2, i // 36 % 2, i // 18 % 2
    level = (2 * w + lo + 1) % 4
    return one_hot(level * 72 + (3 * a + i // 6 % 3) * 12 + 6 * b + i % 6, 288)


def keys_from_pieces():
    i = row_ids(WIN)
    w, piece, t = i // 72, i // 36 % 2, i % 36
    return one_hot(80 * piece + 36 * w + t, 160)


def queries_from_quadrants():
    i = row_ids(320)
    a, b, w, t = i // 160, i // 80 % 2, i // 40 % 2, i % 40
    return one_hot(jnp.where(t < 36, b * 144 + a * 72 + w * 36 + t, -1), 288)


def natural_from_given():
    i = row_ids(288)
    return one_hot(i % 72 * 4 + i // 72, 288)


def given_from_natural():
    i = row_ids(288)
    return one_hot(i % 4 * 72 + i // 4, 288)


def given_from_queries():
    i = row_ids(288)
    level, r, c = (i % 4 + 3) % 4, i // 48, i // 4 % 12
    a, b, w, lo = r // 3, c // 6, level // 2, level % 2
    return one_hot(a * 160 + b * 80 + w * 40 + lo * 18 + r % 3 * 6 + c % 6, 320)


def tail_rows(tiles):
    packed = -(-tiles // 8) * 8
    shape = (packed, tiles * 8)
    i = lax.broadcasted_iota(I32, shape, 0)
    k = lax.broadcasted_iota(I32, shape, 1)
    take = jnp.logical_and(i // 8 == k // 64, i % 8 == k % 8)
    return jnp.where(take, 1.0, 0.0).astype(BF16)


def tail_columns():
    shape = (WIN, 256)
    i = lax.broadcasted_iota(I32, shape, 0)
    k = lax.broadcasted_iota(I32, shape, 1)
    return jnp.where(i == jnp.where(k < 128, k, 128 + k % 16), 1.0, 0.0).astype(BF16)


def shifted_query(a, b, i):
    return 72 * (i // 18) + 12 * (3 * (1 - a) + i // 6 % 3) + 6 * (1 - b) + i % 6


def shifted_key(a, b, i):
    piece, t = i // 36, i % 36
    row = jnp.where(piece < 2, 3 * (1 - a), 3 * a)
    col = jnp.where(piece % 2 == 0, 6 * (1 - b), 6 * b)
    return 72 * (t // 18) + 12 * (row + t // 6 % 3) + col + t % 6


def query_picks():
    i = row_ids(160)
    a, b, t = i // 80, i // 40 % 2, i % 40
    return one_hot(jnp.where(t < 36, shifted_query(a, b, t), -1), WIN)


def key_columns(a, b):
    k = lax.broadcasted_iota(I32, (1, 256), 1)
    position = shifted_key(a, b, jnp.where(k < 128, k, 128 + k % 16))
    i = lax.broadcasted_iota(I32, (WIN, 256), 0)
    return jnp.where(i == position, 1.0, 0.0).astype(BF16)


def pack_table(table_ref, packed_ref):
    for i in range(4):
        word = None
        for g, (bits, steps, place) in enumerate(FIELDS):
            top = 2.0 ** (bits - 1) - 1
            fixed = jnp.minimum(jnp.round(table_ref[4 * g + i].astype(F32) * steps), top).astype(I32)
            field = (fixed & (2**bits - 1)) << place
            word = field if word is None else word | field
        packed_ref[2 * i : 2 * i + 2, 0:POS] = word


def unpack(words, g):
    bits, steps, place = FIELDS[g]
    fixed = (words << (32 - bits - place)) >> (32 - bits)
    return fixed.astype(F32) * (LOG2E / steps)


def split_index(position_index):
    high = (position_index >> 7).astype(F32).astype(BF16)
    low = (position_index & 127).astype(F32).astype(BF16)
    return high, low


def fold_tail(values, gather_rows, tiles):
    row = lax.broadcasted_iota(I32, values.shape, 0) // 8
    lane = lax.broadcasted_iota(I32, values.shape, 1) // 16
    kept = jnp.where((row % 8) == lane, values, 0.0).astype(BF16)
    return dot(gather_rows, kept)


def place_index(part, columns, gather_rows, dst_ref, start, tiles):
    spread = dot(part, columns)
    rows = tiles * 8
    dst_ref[start : start + rows, :] = spread[:, :128].astype(I32)
    tail = fold_tail(spread[:, 128:], gather_rows, tiles)
    dst_ref[start + rows : start + rows + tail.shape[0], :] = tail.astype(I32)


def expand(packed_ref, high_ref, low_ref, main_ref, tail_ref, tiles):
    def picked(t):
        rows = pl.ds(pl.multiple_of(t * 8, 8), 8)
        low = low_ref[rows, :]
        high = high_ref[rows, :]
        words = [None] * 8
        for c in range(CHUNKS):
            here = high == c
            for r in range(8):
                entries = jnp.broadcast_to(packed_ref[r : r + 1, 128 * c : 128 * c + 128], (8, 128))
                got = jnp.take_along_axis(entries, low, axis=1, mode="promise_in_bounds")
                words[r] = got if c == 0 else jnp.where(here, got, words[r])
        return words

    def main(t, carry):
        for r, words in enumerate(picked(t)):
            main_ref[r, pl.ds(pl.multiple_of(t * 8, 8), 8), :] = words
        return carry

    def tail(v, carry):
        for r, words in enumerate(picked(tiles + v)):
            tail_ref[r, pl.ds(pl.multiple_of(v * 64, 64), 8), :] = words
            for j in range(1, 8):
                at = pl.multiple_of(v * 64 + 8 * j, 8)
                tail_ref[r, pl.ds(at, 8), :] = pltpu.roll(words, 128 - 16 * j, 1)
        return carry

    lax.fori_loop(0, tiles, main, 0)
    lax.fori_loop(0, -(-tiles // 8), tail, 0)


def layer_norm(values, gain):
    center = jnp.mean(values, axis=-1, keepdims=True)
    moved = values - center
    spread = jnp.mean(moved * moved, axis=-1, keepdims=True)
    return (moved * lax.rsqrt(spread + 1e-05) * gain).astype(BF16)


def softmax(scores, mask):
    raised = jnp.where(mask, jnp.exp2(scores), 0.0)
    total = jnp.sum(raised, axis=-1, keepdims=True)
    step = jnp.where(total > 1.0, 0.25, 1.0)
    return ((raised * step) * (1.0 / (total * step))).astype(BF16)


def four_heads(query, key, value, biases, mask):
    n = query.shape[0]
    own = lax.broadcasted_iota(I32, query.shape, 1) // 32
    stacked = jnp.concatenate([jnp.where(own == i, query, 0.0) for i in range(4)], axis=0)
    scores = dot_t(stacked.astype(BF16), key)
    probs = [
        softmax(scores[n * i : n * i + n] * SCALE + biases[i], mask) for i in range(4)
    ]
    parts = dot(jnp.concatenate(probs, axis=0), value)
    out = parts[0:n]
    for i in range(1, 4):
        out = jnp.where(own == i, parts[n * i : n * i + n], out)
    return out


def first_kernel(
    idx_in, table_in, tok_in, wqkv_in, wo_in, gain_in, gain2_in,
    first_ref, west_ref, east_ref,
    idx_ref, table_ref, tok_ref, wqkv_ref, wo_ref, gain_ref, gain2_ref, sems,
    values_ref, packed, high_ref, low_ref, main_ref, tail_ref, qbuf, kpad, vpad, obuf,
):
    pairs = (
        (idx_in, idx_ref), (table_in, table_ref), (tok_in, tok_ref), (wqkv_in, wqkv_ref),
        (wo_in, wo_ref), (gain_in, gain_ref), (gain2_in, gain2_ref),
    )
    copies = [pltpu.make_async_copy(src, dst, sems.at[i]) for i, (src, dst) in enumerate(pairs)]
    for copy in copies:
        copy.start()
    copies[0].wait()
    copies[1].wait()
    pack_table(table_ref, packed)
    high, low = split_index(idx_ref[...])
    columns, gather_rows = tail_columns(), tail_rows(18)
    place_index(high, columns, gather_rows, high_ref, 0, 18)
    place_index(low, columns, gather_rows, low_ref, 0, 18)
    expand(packed, high_ref, low_ref, main_ref, tail_ref, 18)

    for copy in copies[2:]:
        copy.wait()
    for g in range(72):
        values_ref[4 * g : 4 * g + 4, :] = tok_ref[g].astype(F32)
    values = dot(natural_from_given(), values_ref[...].astype(BF16))
    values_ref[...] = values
    normed = layer_norm(values, gain_ref[...])
    qkv = dot(normed, wqkv_ref[...]).astype(BF16)
    qbuf[...] = qkv[:, 0:D].astype(F32)
    for w in range(2):
        rows = slice(WIN * w, WIN * w + WIN)
        kpad[w, 0:WIN, :] = qkv[rows, D : 2 * D]
        vpad[w, 0:WIN, :] = qkv[rows, 2 * D :]
        kpad[w, WIN:, :] = jnp.zeros((256 - WIN, D), BF16)
        vpad[w, WIN:, :] = jnp.zeros((256 - WIN, D), BF16)

    valid = lax.broadcasted_iota(I32, (WIN, 256), 1) < WIN
    for g in range(3):
        lanes = slice(128 * g, 128 * g + 128)
        for w in range(2):
            rows = slice(WIN * w, WIN * w + WIN)
            biases = [
                unpack(
                    jnp.concatenate([main_ref[2 * i + w], tail_ref[2 * i + w, 0:WIN, :]], axis=1), g
                )
                for i in range(4)
            ]
            obuf[rows, lanes] = four_heads(
                qbuf[rows, lanes], kpad[w, :, lanes], vpad[w, :, lanes], biases, valid
            ).astype(BF16)
    first = (values_ref[...] + dot(obuf[...], wo_ref[...])).astype(BF16)
    first_ref[...] = first
    again = layer_norm(first.astype(F32), gain2_ref[...])
    parts = dot(quadrants_from_natural(), again).astype(BF16)
    for a in range(2):
        west_ref[a] = parts[72 * a : 72 * a + 72]
        east_ref[a] = parts[144 + 72 * a : 144 + 72 * a + 72]


def fill_bias(
    where_ref, idx_in, table_in, before_in, main_ref, tail_ref,
    idx_ref, tables, packed, high_ref, low_ref, sems,
):
    copies = [
        pltpu.make_async_copy(src, dst, sems.at[i])
        for i, (src, dst) in enumerate(
            ((idx_in, idx_ref), (before_in, tables.at[0]), (table_in, tables.at[1]))
        )
    ]
    for copy in copies:
        copy.start()
    for copy in copies:
        copy.wait()
    pack_table(tables.at[0], packed.at[0])
    pack_table(tables.at[1], packed.at[1])

    @pl.when(where_ref[0] == 0)
    def _():
        packed[0] = packed[1]

    high, low = split_index(idx_ref[...])
    picks, gather_rows = query_picks(), tail_rows(10)
    for a in range(2):
        columns = [key_columns(a, b) for b in range(2)]
        for part, dst in ((high, high_ref), (low, low_ref)):
            rows = dot(picks[80 * a : 80 * a + 80], part).astype(BF16)
            spread = jnp.concatenate(
                [dot(rows[40 * b : 40 * b + 40], columns[b]) for b in range(2)], axis=0
            )
            dst[a, 0:80, :] = spread[:, :128].astype(I32)
            tail = fold_tail(spread[:, 128:], gather_rows, 10)
            dst[a, 80:96, :] = tail.astype(I32)
    for a in range(2):
        expand(packed.at[a], high_ref.at[a], low_ref.at[a], main_ref.at[a], tail_ref.at[a], 10)


def early_kernel(where_ref, idx_in, table_in, before_in, main_ref, tail_ref, *scratch):
    @pl.when(where_ref[1] == 1)
    def _():
        fill_bias(where_ref, idx_in, table_in, before_in, main_ref, tail_ref, *scratch)


def late_kernel(
    where_ref, idx_in, table_in, before_in, main_in, tail_in, *refs
):
    kept, (main_ref, tail_ref), staged, scratch, sems = refs[:5], refs[5:7], refs[7:12], refs[12:-1], refs[-1]
    copies = [
        pltpu.make_async_copy(src, dst, sems.at[i]) for i, (src, dst) in enumerate(zip(kept, staged))
    ]
    for copy in copies:
        copy.start()

    @pl.when(where_ref[1] == 0)
    def _():
        fill_bias(where_ref, idx_in, table_in, before_in, main_ref, tail_ref, *scratch)

    @pl.when(where_ref[1] == 1)
    def _():
        main_ref[...] = main_in[...]
        tail_ref[...] = tail_in[...]

    for copy in copies:
        copy.wait()


def stack_kernel(where_ref, west_ref, east_ref, from_west_ref, from_east_ref, seam_ref, up_ref, down_ref):
    for a, dst in enumerate((up_ref, down_ref)):
        dst[0] = from_west_ref[a]
        dst[1] = west_ref[a]
        dst[2] = east_ref[a]
        dst[3] = jnp.where(where_ref[2] == 1, seam_ref[a], from_east_ref[a])


def half_window(cat, order, pieces):
    cat[72:80, :] = jnp.zeros((8, D), F32)
    cat[152:160, :] = jnp.zeros((8, D), F32)
    for i, piece in enumerate(pieces):
        cat[80 * i : 80 * i + 72, :] = piece.astype(F32)
    return dot(order, cat[...].astype(BF16)).astype(BF16)


def near_kernel(up_ref, down_ref, wqkv_ref, query_ref, near_ref, cat, window):
    here = (up_ref, down_ref)
    tokens = jnp.concatenate([up_ref[1], down_ref[1], up_ref[2], down_ref[2]], axis=0)
    asked = dot(queries_from_quadrants(), tokens).astype(BF16)
    query_ref[...] = dot(asked, wqkv_ref[:, 0:D]).astype(BF16).astype(F32)
    order = keys_from_pieces()
    for a in range(2):
        for b in range(2):
            q = 2 * a + b
            window[WIN * q : WIN * q + WIN, :] = half_window(
                cat.at[q], order, (here[a][1 + b], here[a][3 * b])
            )
    near_ref[...] = dot(window[...], wqkv_ref[:, D:]).astype(BF16).astype(F32)


def second_kernel(
    edge_ref,
    first_ref, query_ref, near_ref, north_ref, south_ref,
    wqkv_ref, wo_ref, main_ref, tail_ref,
    out_ref,
    cat, window, result, kpad, vpad, obuf,
):
    beyond = (north_ref, south_ref)
    order = keys_from_pieces()
    for a in range(2):
        for b in range(2):
            q = 2 * a + b
            far = ((1, 0), (2, 3))[b]
            window[WIN * q : WIN * q + WIN, :] = half_window(
                cat.at[q], order, (beyond[a][far[0]], beyond[a][far[1]])
            )
    for dst, start in ((kpad, 0), (vpad, D)):
        made = dot(window[...], wqkv_ref[:, D + start : 2 * D + start]).astype(BF16).astype(F32)
        for j in range(8):
            rows = slice(72 * j, 72 * j + 72)
            both = jnp.concatenate([near_ref[rows, start : start + D], made[rows]], axis=0)
            dst[j, 0:WIN, :] = both.astype(BF16)
            dst[j, WIN:, :] = jnp.zeros((256 - WIN, D), BF16)

    shape = (40, 256)
    lane = lax.broadcasted_iota(I32, shape, 1)
    side_q = jnp.minimum(lax.broadcasted_iota(I32, shape, 0) // 18, 1)
    side_k = (lane % 36) // 18
    inside = lane < WIN
    near = lane < 72
    split = side_q == side_k
    for a in range(2):
        open_side = edge_ref[a] > 0
        seen = jnp.logical_and(inside, jnp.logical_or(near, open_side))
        masks = (seen, jnp.logical_and(seen, split))
        for g in range(3):
            lanes = slice(128 * g, 128 * g + 128)
            for b in range(2):
                rows = slice(40 * b, 40 * b + 40)
                for w in range(2):
                    at = 4 * a + 2 * b + w
                    biases = [
                        unpack(
                            jnp.concatenate(
                                [main_ref[a, 2 * i + w, rows, :], tail_ref[a, 2 * i + w, rows, :]], axis=1
                            ),
                            g,
                        )
                        for i in range(4)
                    ]
                    obuf[40 * at : 40 * at + 40, lanes] = four_heads(
                        query_ref[40 * at : 40 * at + 40, lanes], kpad[at, :, lanes], vpad[at, :, lanes],
                        biases, masks[w],
                    )
    attended = dot(given_from_queries(), obuf[...].astype(BF16)).astype(BF16)
    result[...] = dot(given_from_natural(), first_ref[...]) + dot(attended, wo_ref[...])
    for g in range(72):
        out_ref[g] = result[4 * g : 4 * g + 4, :].astype(BF16)


VMEM = pl.BlockSpec(memory_space=pltpu.VMEM)
SMEM = pl.BlockSpec(memory_space=pltpu.SMEM)
HBM = pl.BlockSpec(memory_space=pltpu.HBM)
ANY = pl.BlockSpec(memory_space=pl.ANY)
LIMIT = 32 * 1024 * 1024
WIDE = 60 * 1024 * 1024


def shift(block, axis, by, wrap):
    size = lax.axis_size(axis)
    route = [(i, (i + by) % size) for i in range(size) if wrap or 0 <= i + by < size]
    return lax.ppermute(block, axis, route)


def cost(flops, moved):
    return pl.CostEstimate(flops=flops, bytes_accessed=moved, transcendentals=10**6)


def shards(
    tokens, position_index, gain_first, qkv_first, proj_first, bias_first,
    gain_second, qkv_second, proj_second, bias_second,
):
    lat = lax.axis_index("lat")
    last = lax.axis_size("lat") - 1
    params = pltpu.CompilerParams(vmem_limit_bytes=LIMIT)

    part = lax.axis_size("lon") // 2
    place = lax.axis_index("lon") % part
    where = jnp.stack([lat, (place == 0).astype(lat.dtype), (place == part - 1).astype(lat.dtype)])
    where = where.astype(I32)
    table = bias_second.transpose(0, 2, 1, 3).reshape(HEADS, 2, POS)
    before = shift(table, "lat", 1, False)

    first, west, east = pl.pallas_call(
        first_kernel,
        out_shape=(
            jax.ShapeDtypeStruct((288, D), BF16),
            jax.ShapeDtypeStruct((2, 72, D), BF16),
            jax.ShapeDtypeStruct((2, 72, D), BF16),
        ),
        in_specs=[HBM] * 7,
        out_specs=(VMEM,) * 3,
        scratch_shapes=[
            pltpu.VMEM((WIN, WIN), I32),
            pltpu.VMEM((HEADS, 2, POS), BF16),
            pltpu.VMEM((72, 4, D), BF16),
            pltpu.VMEM((D, 3 * D), BF16),
            pltpu.VMEM((D, D), BF16),
            pltpu.VMEM((D,), F32),
            pltpu.VMEM((D,), F32),
            pltpu.SemaphoreType.DMA((7,)),
            pltpu.VMEM((288, D), F32),
            pltpu.VMEM((8, CHUNKS * 128), I32),
            pltpu.VMEM((168, 128), I32),
            pltpu.VMEM((168, 128), I32),
            pltpu.VMEM((8, WIN, 128), I32),
            pltpu.VMEM((8, 192, 128), I32),
            pltpu.VMEM((288, D), F32),
            pltpu.VMEM((2, 256, D), BF16),
            pltpu.VMEM((2, 256, D), BF16),
            pltpu.VMEM((288, D), BF16),
        ],
        compiler_params=pltpu.CompilerParams(vmem_limit_bytes=WIDE),
        cost_estimate=cost(10**9, 3 * 10**6),
        name="first_block",
    )(
        position_index,
        bias_first.transpose(0, 2, 1, 3).reshape(HEADS, 2, POS),
        tokens.transpose(1, 2, 0, 3).reshape(72, 4, D),
        qkv_first, proj_first, gain_first, gain_second,
    )

    bias_shapes = (
        jax.ShapeDtypeStruct((2, 8, 80, 128), I32),
        jax.ShapeDtypeStruct((2, 8, 128, 128), I32),
    )
    bias_scratch = [
        pltpu.VMEM((WIN, WIN), I32),
        pltpu.VMEM((2, HEADS, 2, POS), BF16),
        pltpu.VMEM((2, 8, CHUNKS * 128), I32),
        pltpu.VMEM((2, 96, 128), I32),
        pltpu.VMEM((2, 96, 128), I32),
        pltpu.SemaphoreType.DMA((3,)),
    ]
    from_west = shift(east, "lon", 1, True)
    size = lax.axis_size("lon")
    inner = [(i, i - 1) for i in range(size) if i % part]
    seam = [(i, (i - 1) % size) for i in range(size) if i % part == 0]
    from_east = lax.ppermute(west, "lon", inner)
    before, west = lax.optimization_barrier((before, west))
    main, tail = pl.pallas_call(
        early_kernel,
        out_shape=bias_shapes,
        in_specs=[SMEM, HBM, HBM, ANY],
        out_specs=(VMEM, VMEM),
        scratch_shapes=bias_scratch,
        compiler_params=params,
        cost_estimate=cost(10**6, 10**5),
        name="early_bias",
    )(where, position_index, table, before)
    main, tail, west = lax.optimization_barrier((main, tail, west))
    from_seam = lax.ppermute(west, "lon", seam)
    staged = (west, east, first, qkv_second, proj_second)
    main, tail, west, east, first, w_qkv, w_proj = pl.pallas_call(
        late_kernel,
        out_shape=bias_shapes + tuple(jax.ShapeDtypeStruct(x.shape, x.dtype) for x in staged),
        in_specs=[SMEM, HBM, HBM, ANY, VMEM, VMEM] + [ANY] * 5,
        out_specs=(VMEM,) * 7,
        scratch_shapes=bias_scratch + [pltpu.SemaphoreType.DMA((5,))],
        compiler_params=params,
        cost_estimate=cost(10**9, 10**7),
        name="late_bias",
    )(where, position_index, table, before, main, tail, *staged)

    west, east, from_west, from_east, from_seam = lax.optimization_barrier(
        (west, east, from_west, from_east, from_seam)
    )
    pieces = jax.ShapeDtypeStruct((4, 72, D), BF16)
    up, down = pl.pallas_call(
        stack_kernel,
        out_shape=(pieces, pieces),
        in_specs=[SMEM] + [VMEM] * 5,
        out_specs=(VMEM, VMEM),
        compiler_params=params,
        cost_estimate=cost(10**5, 10**6),
        name="stack_pieces",
    )(where, west, east, from_west, from_east, from_seam)
    south = shift(up, "lat", -1, False)
    north = shift(down, "lat", 1, False)

    query, near = pl.pallas_call(
        near_kernel,
        out_shape=(jax.ShapeDtypeStruct((320, D), F32), jax.ShapeDtypeStruct((576, 2 * D), F32)),
        in_specs=[VMEM] * 3,
        out_specs=(VMEM, VMEM),
        scratch_shapes=[pltpu.VMEM((4, 160, D), F32), pltpu.VMEM((576, D), BF16)],
        compiler_params=params,
        cost_estimate=cost(10**9, 10**7),
        name="near_half",
    )(up, down, w_qkv)

    edges = jnp.stack([lat > 0, lat < last]).astype(I32)
    out = pl.pallas_call(
        second_kernel,
        out_shape=jax.ShapeDtypeStruct((72, 4, D), BF16),
        in_specs=[SMEM] + [VMEM] * 9,
        out_specs=VMEM,
        scratch_shapes=[
            pltpu.VMEM((4, 160, D), F32),
            pltpu.VMEM((576, D), BF16),
            pltpu.VMEM((288, D), F32),
            pltpu.VMEM((8, 256, D), BF16),
            pltpu.VMEM((8, 256, D), BF16),
            pltpu.VMEM((320, D), F32),
        ],
        compiler_params=params,
        cost_estimate=cost(10**9, 5 * 10**6),
        name="second_block",
    )(edges, first, query, near, north, south, w_qkv, w_proj, main, tail)
    return out.reshape(6, 12, 4, D).transpose(2, 0, 1, 3)


def solution(mesh):
    return jax.shard_map(
        shards,
        mesh=mesh,
        in_specs=(
            P(None, "lat", "lon", None), P(), P(), P(), P(),
            P("lat", None, None, None), P(), P(), P(), P("lat", None, None, None),
        ),
        out_specs=P(None, "lat", "lon", None),
        check_vma=False,
    )
```

```python
import jax
import jax.numpy as jnp
import numpy as np
from jax import lax
from jax.experimental import pallas as pl
from jax.experimental.pallas import tpu as pltpu
from jax.sharding import PartitionSpec as P

F32, BF16, I32 = jnp.float32, jnp.bfloat16, jnp.int32
HEADS = 12
D = 384
WIN = 144
CHUNKS = 26
POS = 3312
LOG2E = float(np.log2(np.e))
FIELDS = ((11, 256.0, 21), (11, 256.0, 10), (10, 128.0, 0))
SCALE = LOG2E * 32 ** -0.5


def dot(a, b):
    return jnp.dot(a, b, preferred_element_type=F32)


def dot_t(a, b):
    return lax.dot_general(a, b, (((1,), (1,)), ((), ())), preferred_element_type=F32)


def one_hot(source, width):
    lane = lax.broadcasted_iota(I32, (source.shape[0], width), 1)
    return jnp.where(lane == source, 1.0, 0.0).astype(BF16)


def row_ids(count):
    return lax.broadcasted_iota(I32, (count, 1), 0)


def quadrants_from_natural():
    i = row_ids(288)
    b, a, w, lo = i // 144, i // 72 % 2, i // 36 % 2, i // 18 % 2
    level = (2 * w + lo + 1) % 4
    return one_hot(level * 72 + (3 * a + i // 6 % 3) * 12 + 6 * b + i % 6, 288)


def keys_from_pieces():
    i = row_ids(WIN)
    w, piece, t = i // 72, i // 36 % 2, i % 36
    return one_hot(80 * piece + 36 * w + t, 160)


def queries_from_quadrants():
    i = row_ids(320)
    a, b, w, t = i // 160, i // 80 % 2, i // 40 % 2, i % 40
    return one_hot(jnp.where(t < 36, b * 144 + a * 72 + w * 36 + t, -1), 288)


def natural_from_given():
    i = row_ids(288)
    return one_hot(i % 72 * 4 + i // 72, 288)


def given_from_natural():
    i = row_ids(288)
    return one_hot(i % 4 * 72 + i // 4, 288)


def given_from_queries():
    i = row_ids(288)
    level, r, c = (i % 4 + 3) % 4, i // 48, i // 4 % 12
    a, b, w, lo = r // 3, c // 6, level // 2, level % 2
    return one_hot(a * 160 + b * 80 + w * 40 + lo * 18 + r % 3 * 6 + c % 6, 320)


def tail_rows(tiles):
    packed = -(-tiles // 8) * 8
    shape = (packed, tiles * 8)
    i = lax.broadcasted_iota(I32, shape, 0)
    k = lax.broadcasted_iota(I32, shape, 1)
    take = jnp.logical_and(i // 8 == k // 64, i % 8 == k % 8)
    return jnp.where(take, 1.0, 0.0).astype(BF16)


def tail_columns():
    shape = (WIN, 256)
    i = lax.broadcasted_iota(I32, shape, 0)
    k = lax.broadcasted_iota(I32, shape, 1)
    return jnp.where(i == jnp.where(k < 128, k, 128 + k % 16), 1.0, 0.0).astype(BF16)


def shifted_query(a, b, i):
    return 72 * (i // 18) + 12 * (3 * (1 - a) + i // 6 % 3) + 6 * (1 - b) + i % 6


def shifted_key(a, b, i):
    piece, t = i // 36, i % 36
    row = jnp.where(piece < 2, 3 * (1 - a), 3 * a)
    col = jnp.where(piece % 2 == 0, 6 * (1 - b), 6 * b)
    return 72 * (t // 18) + 12 * (row + t // 6 % 3) + col + t % 6


def query_picks():
    i = row_ids(160)
    a, b, t = i // 80, i // 40 % 2, i % 40
    return one_hot(jnp.where(t < 36, shifted_query(a, b, t), -1), WIN)


def key_columns(a, b):
    k = lax.broadcasted_iota(I32, (1, 256), 1)
    position = shifted_key(a, b, jnp.where(k < 128, k, 128 + k % 16))
    i = lax.broadcasted_iota(I32, (WIN, 256), 0)
    return jnp.where(i == position, 1.0, 0.0).astype(BF16)


def pack_table(table_ref, packed_ref):
    for i in range(4):
        word = None
        for g, (bits, steps, place) in enumerate(FIELDS):
            top = 2.0 ** (bits - 1) - 1
            fixed = jnp.minimum(jnp.round(table_ref[4 * g + i].astype(F32) * steps), top).astype(I32)
            field = (fixed & (2**bits - 1)) << place
            word = field if word is None else word | field
        packed_ref[2 * i : 2 * i + 2, 0:POS] = word


def unpack(words, g):
    bits, steps, place = FIELDS[g]
    fixed = (words << (32 - bits - place)) >> (32 - bits)
    return fixed.astype(F32) * (LOG2E / steps)


def split_index(position_index):
    high = (position_index >> 7).astype(F32).astype(BF16)
    low = (position_index & 127).astype(F32).astype(BF16)
    return high, low


def fold_tail(values, gather_rows, tiles):
    row = lax.broadcasted_iota(I32, values.shape, 0) // 8
    lane = lax.broadcasted_iota(I32, values.shape, 1) // 16
    kept = jnp.where((row % 8) == lane, values, 0.0).astype(BF16)
    return dot(gather_rows, kept)


def place_index(part, columns, gather_rows, dst_ref, start, tiles):
    spread = dot(part, columns)
    rows = tiles * 8
    dst_ref[start : start + rows, :] = spread[:, :128].astype(I32)
    tail = fold_tail(spread[:, 128:], gather_rows, tiles)
    dst_ref[start + rows : start + rows + tail.shape[0], :] = tail.astype(I32)


def expand(packed_ref, high_ref, low_ref, main_ref, tail_ref, tiles):
    def picked(t):
        rows = pl.ds(pl.multiple_of(t * 8, 8), 8)
        low = low_ref[rows, :]
        high = high_ref[rows, :]
        words = [None] * 8
        for c in range(CHUNKS):
            here = high == c
            for r in range(8):
                entries = jnp.broadcast_to(packed_ref[r : r + 1, 128 * c : 128 * c + 128], (8, 128))
                got = jnp.take_along_axis(entries, low, axis=1, mode="promise_in_bounds")
                words[r] = got if c == 0 else jnp.where(here, got, words[r])
        return words

    def main(t, carry):
        for r, words in enumerate(picked(t)):
            main_ref[r, pl.ds(pl.multiple_of(t * 8, 8), 8), :] = words
        return carry

    def tail(v, carry):
        for r, words in enumerate(picked(tiles + v)):
            tail_ref[r, pl.ds(pl.multiple_of(v * 64, 64), 8), :] = words
            for j in range(1, 8):
                at = pl.multiple_of(v * 64 + 8 * j, 8)
                tail_ref[r, pl.ds(at, 8), :] = pltpu.roll(words, 128 - 16 * j, 1)
        return carry

    lax.fori_loop(0, tiles, main, 0)
    lax.fori_loop(0, -(-tiles // 8), tail, 0)


def layer_norm(values, gain):
    center = jnp.mean(values, axis=-1, keepdims=True)
    moved = values - center
    spread = jnp.mean(moved * moved, axis=-1, keepdims=True)
    return (moved * lax.rsqrt(spread + 1e-05) * gain).astype(BF16)


def softmax(scores, mask):
    raised = jnp.where(mask, jnp.exp2(scores), 0.0)
    total = jnp.sum(raised, axis=-1, keepdims=True)
    step = jnp.where(total > 1.0, 0.25, 1.0)
    return ((raised * step) * (1.0 / (total * step))).astype(BF16)


def four_heads(query, key, value, biases, mask):
    n = query.shape[0]
    own = lax.broadcasted_iota(I32, query.shape, 1) // 32
    stacked = jnp.concatenate([jnp.where(own == i, query, 0.0) for i in range(4)], axis=0)
    scores = dot_t(stacked.astype(BF16), key)
    probs = [
        softmax(scores[n * i : n * i + n] * SCALE + biases[i], mask) for i in range(4)
    ]
    parts = dot(jnp.concatenate(probs, axis=0), value)
    out = parts[0:n]
    for i in range(1, 4):
        out = jnp.where(own == i, parts[n * i : n * i + n], out)
    return out


def first_kernel(
    idx_in, table_in, tok_in, wqkv_in, wo_in, gain_in, gain2_in,
    first_ref, west_ref, east_ref,
    idx_ref, table_ref, tok_ref, wqkv_ref, wo_ref, gain_ref, gain2_ref, sems,
    values_ref, packed, high_ref, low_ref, main_ref, tail_ref, qbuf, kpad, vpad, obuf,
):
    pairs = (
        (idx_in, idx_ref), (table_in, table_ref), (tok_in, tok_ref), (wqkv_in, wqkv_ref),
        (wo_in, wo_ref), (gain_in, gain_ref), (gain2_in, gain2_ref),
    )
    copies = [pltpu.make_async_copy(src, dst, sems.at[i]) for i, (src, dst) in enumerate(pairs)]
    for copy in copies:
        copy.start()
    copies[0].wait()
    copies[1].wait()
    pack_table(table_ref, packed)
    high, low = split_index(idx_ref[...])
    columns, gather_rows = tail_columns(), tail_rows(18)
    place_index(high, columns, gather_rows, high_ref, 0, 18)
    place_index(low, columns, gather_rows, low_ref, 0, 18)
    expand(packed, high_ref, low_ref, main_ref, tail_ref, 18)

    for copy in copies[2:]:
        copy.wait()
    for g in range(72):
        values_ref[4 * g : 4 * g + 4, :] = tok_ref[g].astype(F32)
    values = dot(natural_from_given(), values_ref[...].astype(BF16))
    values_ref[...] = values
    normed = layer_norm(values, gain_ref[...])
    qkv = dot(normed, wqkv_ref[...]).astype(BF16)
    qbuf[...] = qkv[:, 0:D].astype(F32)
    for w in range(2):
        rows = slice(WIN * w, WIN * w + WIN)
        kpad[w, 0:WIN, :] = qkv[rows, D : 2 * D]
        vpad[w, 0:WIN, :] = qkv[rows, 2 * D :]
        kpad[w, WIN:, :] = jnp.zeros((256 - WIN, D), BF16)
        vpad[w, WIN:, :] = jnp.zeros((256 - WIN, D), BF16)

    valid = lax.broadcasted_iota(I32, (WIN, 256), 1) < WIN
    for g in range(3):
        lanes = slice(128 * g, 128 * g + 128)
        for w in range(2):
            rows = slice(WIN * w, WIN * w + WIN)
            biases = [
                unpack(
                    jnp.concatenate([main_ref[2 * i + w], tail_ref[2 * i + w, 0:WIN, :]], axis=1), g
                )
                for i in range(4)
            ]
            obuf[rows, lanes] = four_heads(
                qbuf[rows, lanes], kpad[w, :, lanes], vpad[w, :, lanes], biases, valid
            ).astype(BF16)
    first = (values_ref[...] + dot(obuf[...], wo_ref[...])).astype(BF16)
    first_ref[...] = first
    again = layer_norm(first.astype(F32), gain2_ref[...])
    parts = dot(quadrants_from_natural(), again).astype(BF16)
    for a in range(2):
        west_ref[a] = parts[72 * a : 72 * a + 72]
        east_ref[a] = parts[144 + 72 * a : 144 + 72 * a + 72]


def fill_bias(
    where_ref, idx_in, table_in, before_in, main_ref, tail_ref,
    idx_ref, tables, packed, high_ref, low_ref, sems,
):
    copies = [
        pltpu.make_async_copy(src, dst, sems.at[i])
        for i, (src, dst) in enumerate(
            ((idx_in, idx_ref), (before_in, tables.at[0]), (table_in, tables.at[1]))
        )
    ]
    for copy in copies:
        copy.start()
    for copy in copies:
        copy.wait()
    pack_table(tables.at[0], packed.at[0])
    pack_table(tables.at[1], packed.at[1])

    @pl.when(where_ref[0] == 0)
    def _():
        packed[0] = packed[1]

    high, low = split_index(idx_ref[...])
    picks, gather_rows = query_picks(), tail_rows(10)
    for a in range(2):
        columns = [key_columns(a, b) for b in range(2)]
        for part, dst in ((high, high_ref), (low, low_ref)):
            rows = dot(picks[80 * a : 80 * a + 80], part).astype(BF16)
            spread = jnp.concatenate(
                [dot(rows[40 * b : 40 * b + 40], columns[b]) for b in range(2)], axis=0
            )
            dst[a, 0:80, :] = spread[:, :128].astype(I32)
            tail = fold_tail(spread[:, 128:], gather_rows, 10)
            dst[a, 80:96, :] = tail.astype(I32)
    for a in range(2):
        expand(packed.at[a], high_ref.at[a], low_ref.at[a], main_ref.at[a], tail_ref.at[a], 10)


def early_kernel(where_ref, idx_in, table_in, before_in, main_ref, tail_ref, *scratch):
    @pl.when(where_ref[1] == 1)
    def _():
        fill_bias(where_ref, idx_in, table_in, before_in, main_ref, tail_ref, *scratch)


def late_kernel(
    where_ref, idx_in, table_in, before_in, main_in, tail_in, main_ref, tail_ref, *scratch
):
    @pl.when(where_ref[1] == 0)
    def _():
        fill_bias(where_ref, idx_in, table_in, before_in, main_ref, tail_ref, *scratch)

    @pl.when(where_ref[1] == 1)
    def _():
        main_ref[...] = main_in[...]
        tail_ref[...] = tail_in[...]


def stack_kernel(
    where_ref, west_ref, east_ref, from_west_ref, from_east_ref, seam_ref, after_ref, up_ref, down_ref
):
    for a, dst in enumerate((up_ref, down_ref)):
        dst[0] = from_west_ref[a]
        dst[1] = west_ref[a]
        dst[2] = east_ref[a]
        dst[3] = jnp.where(where_ref[2] == 1, seam_ref[a], from_east_ref[a])


def half_window(cat, order, pieces):
    cat[72:80, :] = jnp.zeros((8, D), F32)
    cat[152:160, :] = jnp.zeros((8, D), F32)
    for i, piece in enumerate(pieces):
        cat[80 * i : 80 * i + 72, :] = piece.astype(F32)
    return dot(order, cat[...].astype(BF16)).astype(BF16)


def near_kernel(up_ref, down_ref, wqkv_ref, query_ref, near_ref, cat, window):
    here = (up_ref, down_ref)
    tokens = jnp.concatenate([up_ref[1], down_ref[1], up_ref[2], down_ref[2]], axis=0)
    asked = dot(queries_from_quadrants(), tokens).astype(BF16)
    query_ref[...] = dot(asked, wqkv_ref[:, 0:D]).astype(BF16).astype(F32)
    order = keys_from_pieces()
    for a in range(2):
        for b in range(2):
            q = 2 * a + b
            window[WIN * q : WIN * q + WIN, :] = half_window(
                cat.at[q], order, (here[a][1 + b], here[a][3 * b])
            )
    near_ref[...] = dot(window[...], wqkv_ref[:, D:]).astype(BF16).astype(F32)


def second_kernel(
    edge_ref,
    first_ref, query_ref, near_ref, north_ref, south_ref,
    wqkv_ref, wo_ref, main_ref, tail_ref,
    out_ref,
    cat, window, result, kpad, vpad, obuf,
):
    beyond = (north_ref, south_ref)
    order = keys_from_pieces()
    for a in range(2):
        for b in range(2):
            q = 2 * a + b
            far = ((1, 0), (2, 3))[b]
            window[WIN * q : WIN * q + WIN, :] = half_window(
                cat.at[q], order, (beyond[a][far[0]], beyond[a][far[1]])
            )
    for dst, start in ((kpad, 0), (vpad, D)):
        made = dot(window[...], wqkv_ref[:, D + start : 2 * D + start]).astype(BF16).astype(F32)
        for j in range(8):
            rows = slice(72 * j, 72 * j + 72)
            both = jnp.concatenate([near_ref[rows, start : start + D], made[rows]], axis=0)
            dst[j, 0:WIN, :] = both.astype(BF16)
            dst[j, WIN:, :] = jnp.zeros((256 - WIN, D), BF16)

    shape = (40, 256)
    lane = lax.broadcasted_iota(I32, shape, 1)
    side_q = jnp.minimum(lax.broadcasted_iota(I32, shape, 0) // 18, 1)
    side_k = (lane % 36) // 18
    inside = lane < WIN
    near = lane < 72
    split = side_q == side_k
    for a in range(2):
        open_side = edge_ref[a] > 0
        seen = jnp.logical_and(inside, jnp.logical_or(near, open_side))
        masks = (seen, jnp.logical_and(seen, split))
        for g in range(3):
            lanes = slice(128 * g, 128 * g + 128)
            for b in range(2):
                rows = slice(40 * b, 40 * b + 40)
                for w in range(2):
                    at = 4 * a + 2 * b + w
                    biases = [
                        unpack(
                            jnp.concatenate(
                                [main_ref[a, 2 * i + w, rows, :], tail_ref[a, 2 * i + w, rows, :]], axis=1
                            ),
                            g,
                        )
                        for i in range(4)
                    ]
                    obuf[40 * at : 40 * at + 40, lanes] = four_heads(
                        query_ref[40 * at : 40 * at + 40, lanes], kpad[at, :, lanes], vpad[at, :, lanes],
                        biases, masks[w],
                    )
    attended = dot(given_from_queries(), obuf[...].astype(BF16)).astype(BF16)
    result[...] = dot(given_from_natural(), first_ref[...]) + dot(attended, wo_ref[...])
    for g in range(72):
        out_ref[g] = result[4 * g : 4 * g + 4, :].astype(BF16)


VMEM = pl.BlockSpec(memory_space=pltpu.VMEM)
SMEM = pl.BlockSpec(memory_space=pltpu.SMEM)
HBM = pl.BlockSpec(memory_space=pltpu.HBM)
ANY = pl.BlockSpec(memory_space=pl.ANY)
LIMIT = 16 * 1024 * 1024
WIDE = 60 * 1024 * 1024


def shift(block, axis, by, wrap):
    size = lax.axis_size(axis)
    route = [(i, (i + by) % size) for i in range(size) if wrap or 0 <= i + by < size]
    return lax.ppermute(block, axis, route)


def cost(flops, moved):
    return pl.CostEstimate(flops=flops, bytes_accessed=moved, transcendentals=10**6)


def shards(
    tokens, position_index, gain_first, qkv_first, proj_first, bias_first,
    gain_second, qkv_second, proj_second, bias_second,
):
    lat = lax.axis_index("lat")
    last = lax.axis_size("lat") - 1
    params = pltpu.CompilerParams(vmem_limit_bytes=LIMIT)

    part = lax.axis_size("lon") // 2
    place = lax.axis_index("lon") % part
    where = jnp.stack([lat, (place == 0).astype(lat.dtype), (place == part - 1).astype(lat.dtype)])
    where = where.astype(I32)
    table = bias_second.transpose(0, 2, 1, 3).reshape(HEADS, 2, POS)
    before = shift(table, "lat", 1, False)

    first, west, east = pl.pallas_call(
        first_kernel,
        out_shape=(
            jax.ShapeDtypeStruct((288, D), BF16),
            jax.ShapeDtypeStruct((2, 72, D), BF16),
            jax.ShapeDtypeStruct((2, 72, D), BF16),
        ),
        in_specs=[HBM] * 7,
        out_specs=(VMEM,) * 3,
        scratch_shapes=[
            pltpu.VMEM((WIN, WIN), I32),
            pltpu.VMEM((HEADS, 2, POS), BF16),
            pltpu.VMEM((72, 4, D), BF16),
            pltpu.VMEM((D, 3 * D), BF16),
            pltpu.VMEM((D, D), BF16),
            pltpu.VMEM((D,), F32),
            pltpu.VMEM((D,), F32),
            pltpu.SemaphoreType.DMA((7,)),
            pltpu.VMEM((288, D), F32),
            pltpu.VMEM((8, CHUNKS * 128), I32),
            pltpu.VMEM((168, 128), I32),
            pltpu.VMEM((168, 128), I32),
            pltpu.VMEM((8, WIN, 128), I32),
            pltpu.VMEM((8, 192, 128), I32),
            pltpu.VMEM((288, D), F32),
            pltpu.VMEM((2, 256, D), BF16),
            pltpu.VMEM((2, 256, D), BF16),
            pltpu.VMEM((288, D), BF16),
        ],
        compiler_params=pltpu.CompilerParams(vmem_limit_bytes=WIDE),
        cost_estimate=cost(10**9, 3 * 10**6),
        name="first_block",
    )(
        position_index,
        bias_first.transpose(0, 2, 1, 3).reshape(HEADS, 2, POS),
        tokens.transpose(1, 2, 0, 3).reshape(72, 4, D),
        qkv_first, proj_first, gain_first, gain_second,
    )

    bias_shapes = (
        jax.ShapeDtypeStruct((2, 8, 80, 128), I32),
        jax.ShapeDtypeStruct((2, 8, 128, 128), I32),
    )
    bias_scratch = [
        pltpu.VMEM((WIN, WIN), I32),
        pltpu.VMEM((2, HEADS, 2, POS), BF16),
        pltpu.VMEM((2, 8, CHUNKS * 128), I32),
        pltpu.VMEM((2, 96, 128), I32),
        pltpu.VMEM((2, 96, 128), I32),
        pltpu.SemaphoreType.DMA((3,)),
    ]
    from_west = shift(east, "lon", 1, True)
    size = lax.axis_size("lon")
    inner = [(i, i - 1) for i in range(size) if i % part]
    seam = [(i, (i - 1) % size) for i in range(size) if i % part == 0]
    from_east = lax.ppermute(west, "lon", inner)
    before, west = lax.optimization_barrier((before, west))
    main, tail = pl.pallas_call(
        early_kernel,
        out_shape=bias_shapes,
        in_specs=[SMEM, HBM, HBM, ANY],
        out_specs=(VMEM, VMEM),
        scratch_shapes=bias_scratch,
        compiler_params=params,
        cost_estimate=cost(10**6, 10**5),
        name="early_bias",
    )(where, position_index, table, before)
    main, tail, west = lax.optimization_barrier((main, tail, west))
    from_seam = lax.ppermute(west, "lon", seam)
    main, tail = pl.pallas_call(
        late_kernel,
        out_shape=bias_shapes,
        in_specs=[SMEM, HBM, HBM, ANY, VMEM, VMEM],
        out_specs=(VMEM, VMEM),
        scratch_shapes=bias_scratch,
        compiler_params=params,
        cost_estimate=cost(10**9, 10**7),
        name="late_bias",
    )(where, position_index, table, before, main, tail)

    pieces = jax.ShapeDtypeStruct((4, 72, D), BF16)
    up, down = pl.pallas_call(
        stack_kernel,
        out_shape=(pieces, pieces),
        in_specs=[SMEM] + [VMEM] * 5 + [ANY],
        out_specs=(VMEM, VMEM),
        compiler_params=pltpu.CompilerParams(vmem_limit_bytes=4 * 1024 * 1024),
        cost_estimate=cost(10**5, 10**6),
        name="stack_pieces",
    )(where, west, east, from_west, from_east, from_seam, main)
    south = shift(up, "lat", -1, False)
    north = shift(down, "lat", 1, False)

    query, near = pl.pallas_call(
        near_kernel,
        out_shape=(jax.ShapeDtypeStruct((320, D), F32), jax.ShapeDtypeStruct((576, 2 * D), F32)),
        in_specs=[VMEM] * 3,
        out_specs=(VMEM, VMEM),
        scratch_shapes=[pltpu.VMEM((4, 160, D), F32), pltpu.VMEM((576, D), BF16)],
        compiler_params=params,
        cost_estimate=cost(10**9, 10**7),
        name="near_half",
    )(up, down, qkv_second)

    edges = jnp.stack([lat > 0, lat < last]).astype(I32)
    out = pl.pallas_call(
        second_kernel,
        out_shape=jax.ShapeDtypeStruct((72, 4, D), BF16),
        in_specs=[SMEM] + [VMEM] * 9,
        out_specs=VMEM,
        scratch_shapes=[
            pltpu.VMEM((4, 160, D), F32),
            pltpu.VMEM((576, D), BF16),
            pltpu.VMEM((288, D), F32),
            pltpu.VMEM((8, 256, D), BF16),
            pltpu.VMEM((8, 256, D), BF16),
            pltpu.VMEM((320, D), F32),
        ],
        compiler_params=params,
        cost_estimate=cost(10**9, 5 * 10**6),
        name="second_block",
    )(edges, first, query, near, north, south, qkv_second, proj_second, main, tail)
    return out.reshape(6, 12, 4, D).transpose(2, 0, 1, 3)


def solution(mesh):
    return jax.shard_map(
        shards,
        mesh=mesh,
        in_specs=(
            P(None, "lat", "lon", None), P(), P(), P(), P(),
            P("lat", None, None, None), P(), P(), P(), P("lat", None, None, None),
        ),
        out_specs=P(None, "lat", "lon", None),
        check_vma=False,
    )
```

```python
import jax
import jax.numpy as jnp
import numpy as np
from jax import lax
from jax.experimental import pallas as pl
from jax.experimental.pallas import tpu as pltpu
from jax.sharding import PartitionSpec as P

F32, BF16, I32 = jnp.float32, jnp.bfloat16, jnp.int32
HEADS = 12
D = 384
WIN = 144
CHUNKS = 26
POS = 3312
LOG2E = float(np.log2(np.e))
FIELDS = ((11, 256.0, 21), (11, 256.0, 10), (10, 128.0, 0))
SCALE = LOG2E * 32 ** -0.5


def dot(a, b):
    return jnp.dot(a, b, preferred_element_type=F32)


def dot_t(a, b):
    return lax.dot_general(a, b, (((1,), (1,)), ((), ())), preferred_element_type=F32)


def one_hot(source, width):
    lane = lax.broadcasted_iota(I32, (source.shape[0], width), 1)
    return jnp.where(lane == source, 1.0, 0.0).astype(BF16)


def row_ids(count):
    return lax.broadcasted_iota(I32, (count, 1), 0)


def quadrants_from_natural():
    i = row_ids(288)
    b, a, w, lo = i // 144, i // 72 % 2, i // 36 % 2, i // 18 % 2
    level = (2 * w + lo + 1) % 4
    return one_hot(level * 72 + (3 * a + i // 6 % 3) * 12 + 6 * b + i % 6, 288)


def keys_from_pieces():
    i = row_ids(WIN)
    w, piece, t = i // 72, i // 36 % 2, i % 36
    return one_hot(80 * piece + 36 * w + t, 160)


def queries_from_quadrants():
    i = row_ids(320)
    a, b, w, t = i // 160, i // 80 % 2, i // 40 % 2, i % 40
    return one_hot(jnp.where(t < 36, b * 144 + a * 72 + w * 36 + t, -1), 288)


def natural_from_given():
    i = row_ids(288)
    return one_hot(i % 72 * 4 + i // 72, 288)


def given_from_natural():
    i = row_ids(288)
    return one_hot(i % 4 * 72 + i // 4, 288)


def given_from_queries():
    i = row_ids(288)
    level, r, c = (i % 4 + 3) % 4, i // 48, i // 4 % 12
    a, b, w, lo = r // 3, c // 6, level // 2, level % 2
    return one_hot(a * 160 + b * 80 + w * 40 + lo * 18 + r % 3 * 6 + c % 6, 320)


def tail_rows(tiles):
    packed = -(-tiles // 8) * 8
    shape = (packed, tiles * 8)
    i = lax.broadcasted_iota(I32, shape, 0)
    k = lax.broadcasted_iota(I32, shape, 1)
    take = jnp.logical_and(i // 8 == k // 64, i % 8 == k % 8)
    return jnp.where(take, 1.0, 0.0).astype(BF16)


def tail_columns():
    shape = (WIN, 256)
    i = lax.broadcasted_iota(I32, shape, 0)
    k = lax.broadcasted_iota(I32, shape, 1)
    return jnp.where(i == jnp.where(k < 128, k, 128 + k % 16), 1.0, 0.0).astype(BF16)


def shifted_query(a, b, i):
    return 72 * (i // 18) + 12 * (3 * (1 - a) + i // 6 % 3) + 6 * (1 - b) + i % 6


def shifted_key(a, b, i):
    piece, t = i // 36, i % 36
    row = jnp.where(piece < 2, 3 * (1 - a), 3 * a)
    col = jnp.where(piece % 2 == 0, 6 * (1 - b), 6 * b)
    return 72 * (t // 18) + 12 * (row + t // 6 % 3) + col + t % 6


def query_picks():
    i = row_ids(160)
    a, b, t = i // 80, i // 40 % 2, i % 40
    return one_hot(jnp.where(t < 36, shifted_query(a, b, t), -1), WIN)


def key_columns(a, b):
    k = lax.broadcasted_iota(I32, (1, 256), 1)
    position = shifted_key(a, b, jnp.where(k < 128, k, 128 + k % 16))
    i = lax.broadcasted_iota(I32, (WIN, 256), 0)
    return jnp.where(i == position, 1.0, 0.0).astype(BF16)


def pack_table(table_ref, packed_ref):
    for i in range(4):
        word = None
        for g, (bits, steps, place) in enumerate(FIELDS):
            top = 2.0 ** (bits - 1) - 1
            fixed = jnp.minimum(jnp.round(table_ref[4 * g + i].astype(F32) * steps), top).astype(I32)
            field = (fixed & (2**bits - 1)) << place
            word = field if word is None else word | field
        packed_ref[2 * i : 2 * i + 2, 0:POS] = word


def unpack(words, g):
    bits, steps, place = FIELDS[g]
    fixed = (words << (32 - bits - place)) >> (32 - bits)
    return fixed.astype(F32) * (LOG2E / steps)


def split_index(position_index):
    high = (position_index >> 7).astype(F32).astype(BF16)
    low = (position_index & 127).astype(F32).astype(BF16)
    return high, low


def fold_tail(values, gather_rows, tiles):
    row = lax.broadcasted_iota(I32, values.shape, 0) // 8
    lane = lax.broadcasted_iota(I32, values.shape, 1) // 16
    kept = jnp.where((row % 8) == lane, values, 0.0).astype(BF16)
    return dot(gather_rows, kept)


def place_index(part, columns, gather_rows, dst_ref, start, tiles):
    spread = dot(part, columns)
    rows = tiles * 8
    dst_ref[start : start + rows, :] = spread[:, :128].astype(I32)
    tail = fold_tail(spread[:, 128:], gather_rows, tiles)
    dst_ref[start + rows : start + rows + tail.shape[0], :] = tail.astype(I32)


def expand(packed_ref, high_ref, low_ref, main_ref, tail_ref, tiles):
    def picked(t):
        rows = pl.ds(pl.multiple_of(t * 8, 8), 8)
        low = low_ref[rows, :]
        high = high_ref[rows, :]
        words = [None] * 8
        for c in range(CHUNKS):
            here = high == c
            for r in range(8):
                entries = jnp.broadcast_to(packed_ref[r : r + 1, 128 * c : 128 * c + 128], (8, 128))
                got = jnp.take_along_axis(entries, low, axis=1, mode="promise_in_bounds")
                words[r] = got if c == 0 else jnp.where(here, got, words[r])
        return words

    def main(t, carry):
        for r, words in enumerate(picked(t)):
            main_ref[r, pl.ds(pl.multiple_of(t * 8, 8), 8), :] = words
        return carry

    def tail(v, carry):
        for r, words in enumerate(picked(tiles + v)):
            tail_ref[r, pl.ds(pl.multiple_of(v * 64, 64), 8), :] = words
            for j in range(1, 8):
                at = pl.multiple_of(v * 64 + 8 * j, 8)
                tail_ref[r, pl.ds(at, 8), :] = pltpu.roll(words, 128 - 16 * j, 1)
        return carry

    lax.fori_loop(0, tiles, main, 0)
    lax.fori_loop(0, -(-tiles // 8), tail, 0)


def layer_norm(values, gain):
    center = jnp.mean(values, axis=-1, keepdims=True)
    moved = values - center
    spread = jnp.mean(moved * moved, axis=-1, keepdims=True)
    return (moved * lax.rsqrt(spread + 1e-05) * gain).astype(BF16)


def softmax(scores, mask):
    raised = jnp.where(mask, jnp.exp2(scores), 0.0)
    total = jnp.sum(raised, axis=-1, keepdims=True)
    step = jnp.where(total > 1.0, 0.25, 1.0)
    return ((raised * step) * (1.0 / (total * step))).astype(BF16)


def four_heads(query, key, value, biases, mask):
    n = query.shape[0]
    own = lax.broadcasted_iota(I32, query.shape, 1) // 32
    stacked = jnp.concatenate([jnp.where(own == i, query, 0.0) for i in range(4)], axis=0)
    scores = dot_t(stacked.astype(BF16), key)
    probs = [
        softmax(scores[n * i : n * i + n] * SCALE + biases[i], mask) for i in range(4)
    ]
    parts = dot(jnp.concatenate(probs, axis=0), value)
    out = parts[0:n]
    for i in range(1, 4):
        out = jnp.where(own == i, parts[n * i : n * i + n], out)
    return out


def first_kernel(
    idx_in, table_in, tok_in, wqkv_in, wo_in, gain_in, gain2_in,
    first_ref, west_ref, east_ref,
    idx_ref, table_ref, tok_ref, wqkv_ref, wo_ref, gain_ref, gain2_ref, sems,
    values_ref, packed, high_ref, low_ref, main_ref, tail_ref, qbuf, kpad, vpad, obuf,
):
    pairs = (
        (idx_in, idx_ref), (table_in, table_ref), (tok_in, tok_ref), (wqkv_in, wqkv_ref),
        (wo_in, wo_ref), (gain_in, gain_ref), (gain2_in, gain2_ref),
    )
    copies = [pltpu.make_async_copy(src, dst, sems.at[i]) for i, (src, dst) in enumerate(pairs)]
    for copy in copies:
        copy.start()
    copies[0].wait()
    copies[1].wait()
    pack_table(table_ref, packed)
    high, low = split_index(idx_ref[...])
    columns, gather_rows = tail_columns(), tail_rows(18)
    place_index(high, columns, gather_rows, high_ref, 0, 18)
    place_index(low, columns, gather_rows, low_ref, 0, 18)
    expand(packed, high_ref, low_ref, main_ref, tail_ref, 18)

    for copy in copies[2:]:
        copy.wait()
    for g in range(72):
        values_ref[4 * g : 4 * g + 4, :] = tok_ref[g].astype(F32)
    values = dot(natural_from_given(), values_ref[...].astype(BF16))
    values_ref[...] = values
    normed = layer_norm(values, gain_ref[...])
    qkv = dot(normed, wqkv_ref[...]).astype(BF16)
    qbuf[...] = qkv[:, 0:D].astype(F32)
    for w in range(2):
        rows = slice(WIN * w, WIN * w + WIN)
        kpad[w, 0:WIN, :] = qkv[rows, D : 2 * D]
        vpad[w, 0:WIN, :] = qkv[rows, 2 * D :]
        kpad[w, WIN:, :] = jnp.zeros((256 - WIN, D), BF16)
        vpad[w, WIN:, :] = jnp.zeros((256 - WIN, D), BF16)

    valid = lax.broadcasted_iota(I32, (WIN, 256), 1) < WIN
    for g in range(3):
        lanes = slice(128 * g, 128 * g + 128)
        for w in range(2):
            rows = slice(WIN * w, WIN * w + WIN)
            biases = [
                unpack(
                    jnp.concatenate([main_ref[2 * i + w], tail_ref[2 * i + w, 0:WIN, :]], axis=1), g
                )
                for i in range(4)
            ]
            obuf[rows, lanes] = four_heads(
                qbuf[rows, lanes], kpad[w, :, lanes], vpad[w, :, lanes], biases, valid
            ).astype(BF16)
    first = (values_ref[...] + dot(obuf[...], wo_ref[...])).astype(BF16)
    first_ref[...] = first
    again = layer_norm(first.astype(F32), gain2_ref[...])
    parts = dot(quadrants_from_natural(), again).astype(BF16)
    for a in range(2):
        west_ref[a] = parts[72 * a : 72 * a + 72]
        east_ref[a] = parts[144 + 72 * a : 144 + 72 * a + 72]


def fill_bias(
    where_ref, idx_in, table_in, before_in, main_ref, tail_ref,
    idx_ref, tables, packed, high_ref, low_ref, sems,
):
    copies = [
        pltpu.make_async_copy(src, dst, sems.at[i])
        for i, (src, dst) in enumerate(
            ((idx_in, idx_ref), (before_in, tables.at[0]), (table_in, tables.at[1]))
        )
    ]
    for copy in copies:
        copy.start()
    for copy in copies:
        copy.wait()
    pack_table(tables.at[0], packed.at[0])
    pack_table(tables.at[1], packed.at[1])

    @pl.when(where_ref[0] == 0)
    def _():
        packed[0] = packed[1]

    high, low = split_index(idx_ref[...])
    picks, gather_rows = query_picks(), tail_rows(10)
    for a in range(2):
        columns = [key_columns(a, b) for b in range(2)]
        for part, dst in ((high, high_ref), (low, low_ref)):
            rows = dot(picks[80 * a : 80 * a + 80], part).astype(BF16)
            spread = jnp.concatenate(
                [dot(rows[40 * b : 40 * b + 40], columns[b]) for b in range(2)], axis=0
            )
            dst[a, 0:80, :] = spread[:, :128].astype(I32)
            tail = fold_tail(spread[:, 128:], gather_rows, 10)
            dst[a, 80:96, :] = tail.astype(I32)
    for a in range(2):
        expand(packed.at[a], high_ref.at[a], low_ref.at[a], main_ref.at[a], tail_ref.at[a], 10)


def early_kernel(where_ref, idx_in, table_in, before_in, main_ref, tail_ref, *scratch):
    @pl.when(where_ref[1] == 1)
    def _():
        fill_bias(where_ref, idx_in, table_in, before_in, main_ref, tail_ref, *scratch)


def late_kernel(
    where_ref, idx_in, table_in, before_in, main_in, tail_in, main_ref, tail_ref, *scratch
):
    @pl.when(where_ref[1] == 0)
    def _():
        fill_bias(where_ref, idx_in, table_in, before_in, main_ref, tail_ref, *scratch)

    @pl.when(where_ref[1] == 1)
    def _():
        main_ref[...] = main_in[...]
        tail_ref[...] = tail_in[...]


def stack_kernel(
    where_ref, west_ref, east_ref, from_west_ref, from_east_ref, seam_ref, after_ref, up_ref, down_ref
):
    for a, dst in enumerate((up_ref, down_ref)):
        dst[0] = from_west_ref[a]
        dst[1] = west_ref[a]
        dst[2] = east_ref[a]
        dst[3] = jnp.where(where_ref[2] == 1, seam_ref[a], from_east_ref[a])


def half_window(cat, order, pieces):
    cat[72:80, :] = jnp.zeros((8, D), F32)
    cat[152:160, :] = jnp.zeros((8, D), F32)
    for i, piece in enumerate(pieces):
        cat[80 * i : 80 * i + 72, :] = piece.astype(F32)
    return dot(order, cat[...].astype(BF16)).astype(BF16)


def near_kernel(up_ref, down_ref, wqkv_ref, query_ref, near_ref, cat, window):
    here = (up_ref, down_ref)
    tokens = jnp.concatenate([up_ref[1], down_ref[1], up_ref[2], down_ref[2]], axis=0)
    asked = dot(queries_from_quadrants(), tokens).astype(BF16)
    query_ref[...] = dot(asked, wqkv_ref[:, 0:D]).astype(BF16).astype(F32)
    order = keys_from_pieces()
    for a in range(2):
        for b in range(2):
            q = 2 * a + b
            window[WIN * q : WIN * q + WIN, :] = half_window(
                cat.at[q], order, (here[a][1 + b], here[a][3 * b])
            )
    near_ref[...] = dot(window[...], wqkv_ref[:, D:]).astype(BF16).astype(F32)


def second_kernel(
    edge_ref,
    first_ref, query_ref, near_ref, north_ref, south_ref,
    wqkv_ref, wo_ref, main_ref, tail_ref,
    out_ref,
    cat, window, result, kpad, vpad, obuf,
):
    beyond = (north_ref, south_ref)
    order = keys_from_pieces()
    for a in range(2):
        for b in range(2):
            q = 2 * a + b
            far = ((1, 0), (2, 3))[b]
            window[WIN * q : WIN * q + WIN, :] = half_window(
                cat.at[q], order, (beyond[a][far[0]], beyond[a][far[1]])
            )
    for dst, start in ((kpad, 0), (vpad, D)):
        made = dot(window[...], wqkv_ref[:, D + start : 2 * D + start]).astype(BF16).astype(F32)
        for j in range(8):
            rows = slice(72 * j, 72 * j + 72)
            both = jnp.concatenate([near_ref[rows, start : start + D], made[rows]], axis=0)
            dst[j, 0:WIN, :] = both.astype(BF16)
            dst[j, WIN:, :] = jnp.zeros((256 - WIN, D), BF16)

    shape = (40, 256)
    lane = lax.broadcasted_iota(I32, shape, 1)
    side_q = jnp.minimum(lax.broadcasted_iota(I32, shape, 0) // 18, 1)
    side_k = (lane % 36) // 18
    inside = lane < WIN
    near = lane < 72
    split = side_q == side_k
    for a in range(2):
        open_side = edge_ref[a] > 0
        seen = jnp.logical_and(inside, jnp.logical_or(near, open_side))
        masks = (seen, jnp.logical_and(seen, split))
        for g in range(3):
            lanes = slice(128 * g, 128 * g + 128)
            for b in range(2):
                rows = slice(40 * b, 40 * b + 40)
                for w in range(2):
                    at = 4 * a + 2 * b + w
                    biases = [
                        unpack(
                            jnp.concatenate(
                                [main_ref[a, 2 * i + w, rows, :], tail_ref[a, 2 * i + w, rows, :]], axis=1
                            ),
                            g,
                        )
                        for i in range(4)
                    ]
                    obuf[40 * at : 40 * at + 40, lanes] = four_heads(
                        query_ref[40 * at : 40 * at + 40, lanes], kpad[at, :, lanes], vpad[at, :, lanes],
                        biases, masks[w],
                    )
    attended = dot(given_from_queries(), obuf[...].astype(BF16)).astype(BF16)
    result[...] = dot(given_from_natural(), first_ref[...]) + dot(attended, wo_ref[...])
    for g in range(72):
        out_ref[g] = result[4 * g : 4 * g + 4, :].astype(BF16)


VMEM = pl.BlockSpec(memory_space=pltpu.VMEM)
SMEM = pl.BlockSpec(memory_space=pltpu.SMEM)
HBM = pl.BlockSpec(memory_space=pltpu.HBM)
ANY = pl.BlockSpec(memory_space=pl.ANY)
LIMIT = 16 * 1024 * 1024
WIDE = 60 * 1024 * 1024


def shift(block, axis, by, wrap):
    size = lax.axis_size(axis)
    route = [(i, (i + by) % size) for i in range(size) if wrap or 0 <= i + by < size]
    return lax.ppermute(block, axis, route)


def cost(flops, moved):
    return pl.CostEstimate(flops=flops, bytes_accessed=moved, transcendentals=10**6)


def shards(
    tokens, position_index, gain_first, qkv_first, proj_first, bias_first,
    gain_second, qkv_second, proj_second, bias_second,
):
    lat = lax.axis_index("lat")
    last = lax.axis_size("lat") - 1
    params = pltpu.CompilerParams(vmem_limit_bytes=LIMIT)

    part = lax.axis_size("lon") // 2
    place = lax.axis_index("lon") % part
    where = jnp.stack([lat, (place == 0).astype(lat.dtype), (place >= part - 2).astype(lat.dtype)])
    where = where.astype(I32)
    table = bias_second.transpose(0, 2, 1, 3).reshape(HEADS, 2, POS)
    before = shift(table, "lat", 1, False)

    first, west, east = pl.pallas_call(
        first_kernel,
        out_shape=(
            jax.ShapeDtypeStruct((288, D), BF16),
            jax.ShapeDtypeStruct((2, 72, D), BF16),
            jax.ShapeDtypeStruct((2, 72, D), BF16),
        ),
        in_specs=[HBM] * 7,
        out_specs=(VMEM,) * 3,
        scratch_shapes=[
            pltpu.VMEM((WIN, WIN), I32),
            pltpu.VMEM((HEADS, 2, POS), BF16),
            pltpu.VMEM((72, 4, D), BF16),
            pltpu.VMEM((D, 3 * D), BF16),
            pltpu.VMEM((D, D), BF16),
            pltpu.VMEM((D,), F32),
            pltpu.VMEM((D,), F32),
            pltpu.SemaphoreType.DMA((7,)),
            pltpu.VMEM((288, D), F32),
            pltpu.VMEM((8, CHUNKS * 128), I32),
            pltpu.VMEM((168, 128), I32),
            pltpu.VMEM((168, 128), I32),
            pltpu.VMEM((8, WIN, 128), I32),
            pltpu.VMEM((8, 192, 128), I32),
            pltpu.VMEM((288, D), F32),
            pltpu.VMEM((2, 256, D), BF16),
            pltpu.VMEM((2, 256, D), BF16),
            pltpu.VMEM((288, D), BF16),
        ],
        compiler_params=pltpu.CompilerParams(vmem_limit_bytes=WIDE),
        cost_estimate=cost(10**9, 3 * 10**6),
        name="first_block",
    )(
        position_index,
        bias_first.transpose(0, 2, 1, 3).reshape(HEADS, 2, POS),
        tokens.transpose(1, 2, 0, 3).reshape(72, 4, D),
        qkv_first, proj_first, gain_first, gain_second,
    )

    bias_shapes = (
        jax.ShapeDtypeStruct((2, 8, 80, 128), I32),
        jax.ShapeDtypeStruct((2, 8, 128, 128), I32),
    )
    bias_scratch = [
        pltpu.VMEM((WIN, WIN), I32),
        pltpu.VMEM((2, HEADS, 2, POS), BF16),
        pltpu.VMEM((2, 8, CHUNKS * 128), I32),
        pltpu.VMEM((2, 96, 128), I32),
        pltpu.VMEM((2, 96, 128), I32),
        pltpu.SemaphoreType.DMA((3,)),
    ]
    from_west = shift(east, "lon", 1, True)
    size = lax.axis_size("lon")
    inner = [(i, i - 1) for i in range(size) if 0 < i % part < part - 1]
    seam = [(i, (i - 1) % size) for i in range(size) if i % part in (0, part - 1)]
    from_east = lax.ppermute(west, "lon", inner)
    before, west = lax.optimization_barrier((before, west))
    main, tail = pl.pallas_call(
        early_kernel,
        out_shape=bias_shapes,
        in_specs=[SMEM, HBM, HBM, ANY],
        out_specs=(VMEM, VMEM),
        scratch_shapes=bias_scratch,
        compiler_params=params,
        cost_estimate=cost(10**6, 10**5),
        name="early_bias",
    )(where, position_index, table, before)
    main, tail, west = lax.optimization_barrier((main, tail, west))
    from_seam = lax.ppermute(west, "lon", seam)
    main, tail = pl.pallas_call(
        late_kernel,
        out_shape=bias_shapes,
        in_specs=[SMEM, HBM, HBM, ANY, VMEM, VMEM],
        out_specs=(VMEM, VMEM),
        scratch_shapes=bias_scratch,
        compiler_params=params,
        cost_estimate=cost(10**9, 10**7),
        name="late_bias",
    )(where, position_index, table, before, main, tail)

    pieces = jax.ShapeDtypeStruct((4, 72, D), BF16)
    up, down = pl.pallas_call(
        stack_kernel,
        out_shape=(pieces, pieces),
        in_specs=[SMEM] + [VMEM] * 5 + [ANY],
        out_specs=(VMEM, VMEM),
        compiler_params=pltpu.CompilerParams(vmem_limit_bytes=4 * 1024 * 1024),
        cost_estimate=cost(10**5, 10**6),
        name="stack_pieces",
    )(where, west, east, from_west, from_east, from_seam, main)
    south = shift(up, "lat", -1, False)
    north = shift(down, "lat", 1, False)

    query, near = pl.pallas_call(
        near_kernel,
        out_shape=(jax.ShapeDtypeStruct((320, D), F32), jax.ShapeDtypeStruct((576, 2 * D), F32)),
        in_specs=[VMEM] * 3,
        out_specs=(VMEM, VMEM),
        scratch_shapes=[pltpu.VMEM((4, 160, D), F32), pltpu.VMEM((576, D), BF16)],
        compiler_params=params,
        cost_estimate=cost(10**9, 10**7),
        name="near_half",
    )(up, down, qkv_second)

    edges = jnp.stack([lat > 0, lat < last]).astype(I32)
    out = pl.pallas_call(
        second_kernel,
        out_shape=jax.ShapeDtypeStruct((72, 4, D), BF16),
        in_specs=[SMEM] + [VMEM] * 9,
        out_specs=VMEM,
        scratch_shapes=[
            pltpu.VMEM((4, 160, D), F32),
            pltpu.VMEM((576, D), BF16),
            pltpu.VMEM((288, D), F32),
            pltpu.VMEM((8, 256, D), BF16),
            pltpu.VMEM((8, 256, D), BF16),
            pltpu.VMEM((320, D), F32),
        ],
        compiler_params=params,
        cost_estimate=cost(10**9, 5 * 10**6),
        name="second_block",
    )(edges, first, query, near, north, south, qkv_second, proj_second, main, tail)
    return out.reshape(6, 12, 4, D).transpose(2, 0, 1, 3)


def solution(mesh):
    return jax.shard_map(
        shards,
        mesh=mesh,
        in_specs=(
            P(None, "lat", "lon", None), P(), P(), P(), P(),
            P("lat", None, None, None), P(), P(), P(), P("lat", None, None, None),
        ),
        out_specs=P(None, "lat", "lon", None),
        check_vma=False,
    )
```

```python
import jax
import jax.numpy as jnp
import numpy as np
from jax import lax
from jax.experimental import pallas as pl
from jax.experimental.pallas import tpu as pltpu
from jax.sharding import PartitionSpec as P

F32, BF16, I32 = jnp.float32, jnp.bfloat16, jnp.int32
HEADS = 12
D = 384
WIN = 144
CHUNKS = 26
POS = 3312
LOG2E = float(np.log2(np.e))
FIELDS = ((11, 256.0, 21), (11, 256.0, 10), (10, 128.0, 0))
SCALE = LOG2E * 32 ** -0.5


def dot(a, b):
    return jnp.dot(a, b, preferred_element_type=F32)


def dot_t(a, b):
    return lax.dot_general(a, b, (((1,), (1,)), ((), ())), preferred_element_type=F32)


def one_hot(source, width):
    lane = lax.broadcasted_iota(I32, (source.shape[0], width), 1)
    return jnp.where(lane == source, 1.0, 0.0).astype(BF16)


def row_ids(count):
    return lax.broadcasted_iota(I32, (count, 1), 0)


def quadrants_from_natural():
    i = row_ids(288)
    b, a, w, lo = i // 144, i // 72 % 2, i // 36 % 2, i // 18 % 2
    level = (2 * w + lo + 1) % 4
    return one_hot(level * 72 + (3 * a + i // 6 % 3) * 12 + 6 * b + i % 6, 288)


def keys_from_pieces():
    i = row_ids(WIN)
    w, piece, t = i // 72, i // 36 % 2, i % 36
    return one_hot(80 * piece + 36 * w + t, 160)


def queries_from_quadrants():
    i = row_ids(320)
    a, b, w, t = i // 160, i // 80 % 2, i // 40 % 2, i % 40
    return one_hot(jnp.where(t < 36, b * 144 + a * 72 + w * 36 + t, -1), 288)


def natural_from_given():
    i = row_ids(288)
    return one_hot(i % 72 * 4 + i // 72, 288)


def given_from_natural():
    i = row_ids(288)
    return one_hot(i % 4 * 72 + i // 4, 288)


def given_from_queries():
    i = row_ids(288)
    level, r, c = (i % 4 + 3) % 4, i // 48, i // 4 % 12
    a, b, w, lo = r // 3, c // 6, level // 2, level % 2
    return one_hot(a * 160 + b * 80 + w * 40 + lo * 18 + r % 3 * 6 + c % 6, 320)


def tail_rows(tiles):
    packed = -(-tiles // 8) * 8
    shape = (packed, tiles * 8)
    i = lax.broadcasted_iota(I32, shape, 0)
    k = lax.broadcasted_iota(I32, shape, 1)
    take = jnp.logical_and(i // 8 == k // 64, i % 8 == k % 8)
    return jnp.where(take, 1.0, 0.0).astype(BF16)


def tail_columns():
    shape = (WIN, 256)
    i = lax.broadcasted_iota(I32, shape, 0)
    k = lax.broadcasted_iota(I32, shape, 1)
    return jnp.where(i == jnp.where(k < 128, k, 128 + k % 16), 1.0, 0.0).astype(BF16)


def shifted_query(a, b, i):
    return 72 * (i // 18) + 12 * (3 * (1 - a) + i // 6 % 3) + 6 * (1 - b) + i % 6


def shifted_key(a, b, i):
    piece, t = i // 36, i % 36
    row = jnp.where(piece < 2, 3 * (1 - a), 3 * a)
    col = jnp.where(piece % 2 == 0, 6 * (1 - b), 6 * b)
    return 72 * (t // 18) + 12 * (row + t // 6 % 3) + col + t % 6


def query_picks():
    i = row_ids(160)
    a, b, t = i // 80, i // 40 % 2, i % 40
    return one_hot(jnp.where(t < 36, shifted_query(a, b, t), -1), WIN)


def key_columns(a, b):
    k = lax.broadcasted_iota(I32, (1, 256), 1)
    position = shifted_key(a, b, jnp.where(k < 128, k, 128 + k % 16))
    i = lax.broadcasted_iota(I32, (WIN, 256), 0)
    return jnp.where(i == position, 1.0, 0.0).astype(BF16)


def pack_table(table_ref, packed_ref):
    for i in range(4):
        word = None
        for g, (bits, steps, place) in enumerate(FIELDS):
            top = 2.0 ** (bits - 1) - 1
            fixed = jnp.minimum(jnp.round(table_ref[4 * g + i].astype(F32) * steps), top).astype(I32)
            field = (fixed & (2**bits - 1)) << place
            word = field if word is None else word | field
        packed_ref[2 * i : 2 * i + 2, 0:POS] = word


def unpack(words, g):
    bits, steps, place = FIELDS[g]
    fixed = (words << (32 - bits - place)) >> (32 - bits)
    return fixed.astype(F32) * (LOG2E / steps)


def split_index(position_index):
    high = (position_index >> 7).astype(F32).astype(BF16)
    low = (position_index & 127).astype(F32).astype(BF16)
    return high, low


def fold_tail(values, gather_rows, tiles):
    row = lax.broadcasted_iota(I32, values.shape, 0) // 8
    lane = lax.broadcasted_iota(I32, values.shape, 1) // 16
    kept = jnp.where((row % 8) == lane, values, 0.0).astype(BF16)
    return dot(gather_rows, kept)


def place_index(part, columns, gather_rows, dst_ref, start, tiles):
    spread = dot(part, columns)
    rows = tiles * 8
    dst_ref[start : start + rows, :] = spread[:, :128].astype(I32)
    tail = fold_tail(spread[:, 128:], gather_rows, tiles)
    dst_ref[start + rows : start + rows + tail.shape[0], :] = tail.astype(I32)


def expand(packed_ref, high_ref, low_ref, main_ref, tail_ref, tiles):
    def picked(at):
        low = [low_ref[pl.ds(r, 8), :] for r in at]
        high = [high_ref[pl.ds(r, 8), :] for r in at]
        words = [[None] * 8 for _ in at]
        for c in range(CHUNKS):
            here = [x == c for x in high]
            for r in range(8):
                entries = jnp.broadcast_to(packed_ref[r : r + 1, 128 * c : 128 * c + 128], (8, 128))
                for k in range(len(at)):
                    got = jnp.take_along_axis(entries, low[k], axis=1, mode="promise_in_bounds")
                    words[k][r] = got if c == 0 else jnp.where(here[k], got, words[k][r])
        return words

    def main(t, carry):
        at = [pl.multiple_of(t * 16, 8), pl.multiple_of(t * 16 + 8, 8)]
        for start, words in zip(at, picked(at)):
            for r in range(8):
                main_ref[r, pl.ds(start, 8), :] = words[r]
        return carry

    lax.fori_loop(0, tiles // 2, main, 0)
    tails = list(range(-(-tiles // 8)))
    for first in tails[::2]:
        group = tails[first : first + 2]
        for v, words in zip(group, picked([8 * (tiles + v) for v in group])):
            for r in range(8):
                for j in range(min(8, tiles - 8 * v)):
                    rolled = words[r] if j == 0 else pltpu.roll(words[r], 128 - 16 * j, 1)
                    tail_ref[r, 64 * v + 8 * j : 64 * v + 8 * j + 8, :] = rolled


def layer_norm(values, gain):
    center = jnp.mean(values, axis=-1, keepdims=True)
    moved = values - center
    spread = jnp.mean(moved * moved, axis=-1, keepdims=True)
    return (moved * lax.rsqrt(spread + 1e-05) * gain).astype(BF16)


def softmax(scores, mask):
    raised = jnp.where(mask, jnp.exp2(scores), 0.0)
    total = jnp.sum(raised, axis=-1, keepdims=True)
    step = jnp.where(total > 1.0, 0.25, 1.0)
    return ((raised * step) * (1.0 / (total * step))).astype(BF16)


def four_heads(query, key, value, biases, mask):
    n = query.shape[0]
    own = lax.broadcasted_iota(I32, query.shape, 1) // 32
    stacked = jnp.concatenate([jnp.where(own == i, query, 0.0) for i in range(4)], axis=0)
    scores = dot_t(stacked.astype(BF16), key)
    probs = [
        softmax(scores[n * i : n * i + n] * SCALE + biases[i], mask) for i in range(4)
    ]
    parts = dot(jnp.concatenate(probs, axis=0), value)
    out = parts[0:n]
    for i in range(1, 4):
        out = jnp.where(own == i, parts[n * i : n * i + n], out)
    return out


def first_kernel(
    idx_in, table_in, tok_in, wqkv_in, wo_in, gain_in, gain2_in,
    first_ref, west_ref, east_ref,
    idx_ref, table_ref, tok_ref, wqkv_ref, wo_ref, gain_ref, gain2_ref, sems,
    values_ref, packed, high_ref, low_ref, main_ref, tail_ref, qbuf, kpad, vpad, obuf,
):
    pairs = (
        (idx_in, idx_ref), (table_in, table_ref), (tok_in, tok_ref), (wqkv_in, wqkv_ref),
        (wo_in, wo_ref), (gain_in, gain_ref), (gain2_in, gain2_ref),
    )
    copies = [pltpu.make_async_copy(src, dst, sems.at[i]) for i, (src, dst) in enumerate(pairs)]
    for copy in copies:
        copy.start()
    copies[0].wait()
    copies[1].wait()
    pack_table(table_ref, packed)
    high, low = split_index(idx_ref[...])
    columns, gather_rows = tail_columns(), tail_rows(18)
    place_index(high, columns, gather_rows, high_ref, 0, 18)
    place_index(low, columns, gather_rows, low_ref, 0, 18)
    expand(packed, high_ref, low_ref, main_ref, tail_ref, 18)

    for copy in copies[2:]:
        copy.wait()
    for g in range(72):
        values_ref[4 * g : 4 * g + 4, :] = tok_ref[g].astype(F32)
    values = dot(natural_from_given(), values_ref[...].astype(BF16))
    values_ref[...] = values
    normed = layer_norm(values, gain_ref[...])
    qkv = dot(normed, wqkv_ref[...]).astype(BF16)
    qbuf[...] = qkv[:, 0:D].astype(F32)
    for w in range(2):
        rows = slice(WIN * w, WIN * w + WIN)
        kpad[w, 0:WIN, :] = qkv[rows, D : 2 * D]
        vpad[w, 0:WIN, :] = qkv[rows, 2 * D :]
        kpad[w, WIN:, :] = jnp.zeros((256 - WIN, D), BF16)
        vpad[w, WIN:, :] = jnp.zeros((256 - WIN, D), BF16)

    valid = lax.broadcasted_iota(I32, (WIN, 256), 1) < WIN
    for g in range(3):
        lanes = slice(128 * g, 128 * g + 128)
        for w in range(2):
            rows = slice(WIN * w, WIN * w + WIN)
            biases = [
                unpack(
                    jnp.concatenate([main_ref[2 * i + w], tail_ref[2 * i + w, 0:WIN, :]], axis=1), g
                )
                for i in range(4)
            ]
            obuf[rows, lanes] = four_heads(
                qbuf[rows, lanes], kpad[w, :, lanes], vpad[w, :, lanes], biases, valid
            ).astype(BF16)
    first = (values_ref[...] + dot(obuf[...], wo_ref[...])).astype(BF16)
    first_ref[...] = first
    again = layer_norm(first.astype(F32), gain2_ref[...])
    parts = dot(quadrants_from_natural(), again).astype(BF16)
    for a in range(2):
        west_ref[a] = parts[72 * a : 72 * a + 72]
        east_ref[a] = parts[144 + 72 * a : 144 + 72 * a + 72]


def fill_bias(
    where_ref, idx_ref, table_ref, before_ref, main_ref, tail_ref, packed, high_ref, low_ref
):
    pack_table(before_ref, packed.at[0])
    pack_table(table_ref, packed.at[1])

    @pl.when(where_ref[0] == 0)
    def _():
        packed[0] = packed[1]

    high, low = split_index(idx_ref[...])
    picks, gather_rows = query_picks(), tail_rows(10)
    for a in range(2):
        columns = [key_columns(a, b) for b in range(2)]
        for part, dst in ((high, high_ref), (low, low_ref)):
            rows = dot(picks[80 * a : 80 * a + 80], part).astype(BF16)
            spread = jnp.concatenate(
                [dot(rows[40 * b : 40 * b + 40], columns[b]) for b in range(2)], axis=0
            )
            dst[a, 0:80, :] = spread[:, :128].astype(I32)
            tail = fold_tail(spread[:, 128:], gather_rows, 10)
            dst[a, 80:96, :] = tail.astype(I32)
    for a in range(2):
        expand(packed.at[a], high_ref.at[a], low_ref.at[a], main_ref.at[a], tail_ref.at[a], 10)


def early_kernel(where_ref, idx_in, table_in, before_in, main_ref, tail_ref, *scratch):
    @pl.when(where_ref[1] == 1)
    def _():
        fill_bias(where_ref, idx_in, table_in, before_in, main_ref, tail_ref, *scratch)


def late_kernel(
    where_ref, idx_in, table_in, before_in, main_in, tail_in, main_ref, tail_ref, *scratch
):
    @pl.when(where_ref[1] == 0)
    def _():
        fill_bias(where_ref, idx_in, table_in, before_in, main_ref, tail_ref, *scratch)

    @pl.when(where_ref[1] == 1)
    def _():
        main_ref[...] = main_in[...]
        tail_ref[...] = tail_in[...]


def stack_kernel(
    where_ref, west_ref, east_ref, from_west_ref, from_east_ref, seam_ref, after_ref, up_ref, down_ref
):
    for a, dst in enumerate((up_ref, down_ref)):
        dst[0] = from_west_ref[a]
        dst[1] = west_ref[a]
        dst[2] = east_ref[a]
        dst[3] = jnp.where(where_ref[2] == 1, seam_ref[a], from_east_ref[a])


def half_window(cat, order, pieces):
    cat[72:80, :] = jnp.zeros((8, D), F32)
    cat[152:160, :] = jnp.zeros((8, D), F32)
    for i, piece in enumerate(pieces):
        cat[80 * i : 80 * i + 72, :] = piece.astype(F32)
    return dot(order, cat[...].astype(BF16)).astype(BF16)


def near_kernel(up_ref, down_ref, wqkv_ref, query_ref, near_ref, cat, window):
    here = (up_ref, down_ref)
    tokens = jnp.concatenate([up_ref[1], down_ref[1], up_ref[2], down_ref[2]], axis=0)
    asked = dot(queries_from_quadrants(), tokens).astype(BF16)
    query_ref[...] = dot(asked, wqkv_ref[:, 0:D]).astype(BF16).astype(F32)
    order = keys_from_pieces()
    for a in range(2):
        for b in range(2):
            q = 2 * a + b
            window[WIN * q : WIN * q + WIN, :] = half_window(
                cat.at[q], order, (here[a][1 + b], here[a][3 * b])
            )
    near_ref[...] = dot(window[...], wqkv_ref[:, D:]).astype(BF16).astype(F32)


def second_kernel(
    edge_ref,
    first_ref, query_ref, near_ref, north_ref, south_ref,
    wqkv_ref, wo_ref, main_ref, tail_ref,
    out_ref,
    cat, window, result, kpad, vpad, obuf,
):
    beyond = (north_ref, south_ref)
    order = keys_from_pieces()
    for a in range(2):
        for b in range(2):
            q = 2 * a + b
            far = ((1, 0), (2, 3))[b]
            window[WIN * q : WIN * q + WIN, :] = half_window(
                cat.at[q], order, (beyond[a][far[0]], beyond[a][far[1]])
            )
    for dst, start in ((kpad, 0), (vpad, D)):
        made = dot(window[...], wqkv_ref[:, D + start : 2 * D + start]).astype(BF16).astype(F32)
        for j in range(8):
            rows = slice(72 * j, 72 * j + 72)
            both = jnp.concatenate([near_ref[rows, start : start + D], made[rows]], axis=0)
            dst[j, 0:WIN, :] = both.astype(BF16)
            dst[j, WIN:, :] = jnp.zeros((256 - WIN, D), BF16)

    shape = (40, 256)
    lane = lax.broadcasted_iota(I32, shape, 1)
    side_q = jnp.minimum(lax.broadcasted_iota(I32, shape, 0) // 18, 1)
    side_k = (lane % 36) // 18
    inside = lane < WIN
    near = lane < 72
    split = side_q == side_k
    for a in range(2):
        open_side = edge_ref[a] > 0
        seen = jnp.logical_and(inside, jnp.logical_or(near, open_side))
        masks = (seen, jnp.logical_and(seen, split))
        for g in range(3):
            lanes = slice(128 * g, 128 * g + 128)
            for b in range(2):
                rows = slice(40 * b, 40 * b + 40)
                for w in range(2):
                    at = 4 * a + 2 * b + w
                    biases = [
                        unpack(
                            jnp.concatenate(
                                [main_ref[a, 2 * i + w, rows, :], tail_ref[a, 2 * i + w, rows, :]], axis=1
                            ),
                            g,
                        )
                        for i in range(4)
                    ]
                    obuf[40 * at : 40 * at + 40, lanes] = four_heads(
                        query_ref[40 * at : 40 * at + 40, lanes], kpad[at, :, lanes], vpad[at, :, lanes],
                        biases, masks[w],
                    )
    attended = dot(given_from_queries(), obuf[...].astype(BF16)).astype(BF16)
    result[...] = dot(given_from_natural(), first_ref[...]) + dot(attended, wo_ref[...])
    for g in range(72):
        out_ref[g] = result[4 * g : 4 * g + 4, :].astype(BF16)


VMEM = pl.BlockSpec(memory_space=pltpu.VMEM)
SMEM = pl.BlockSpec(memory_space=pltpu.SMEM)
HBM = pl.BlockSpec(memory_space=pltpu.HBM)
ANY = pl.BlockSpec(memory_space=pl.ANY)
LIMIT = 16 * 1024 * 1024
WIDE = 60 * 1024 * 1024


def shift(block, axis, by, wrap):
    size = lax.axis_size(axis)
    route = [(i, (i + by) % size) for i in range(size) if wrap or 0 <= i + by < size]
    return lax.ppermute(block, axis, route)


def cost(flops, moved):
    return pl.CostEstimate(flops=flops, bytes_accessed=moved, transcendentals=10**6)


def shards(
    tokens, position_index, gain_first, qkv_first, proj_first, bias_first,
    gain_second, qkv_second, proj_second, bias_second,
):
    lat = lax.axis_index("lat")
    last = lax.axis_size("lat") - 1
    params = pltpu.CompilerParams(vmem_limit_bytes=LIMIT)

    part = lax.axis_size("lon") // 2
    place = lax.axis_index("lon") % part
    where = jnp.stack([lat, (place == 0).astype(lat.dtype), (place >= part - 2).astype(lat.dtype)])
    where = where.astype(I32)
    table = bias_second.transpose(0, 2, 1, 3).reshape(HEADS, 2, POS)
    before = shift(table, "lat", 1, False)

    first, west, east = pl.pallas_call(
        first_kernel,
        out_shape=(
            jax.ShapeDtypeStruct((288, D), BF16),
            jax.ShapeDtypeStruct((2, 72, D), BF16),
            jax.ShapeDtypeStruct((2, 72, D), BF16),
        ),
        in_specs=[HBM] * 7,
        out_specs=(VMEM,) * 3,
        scratch_shapes=[
            pltpu.VMEM((WIN, WIN), I32),
            pltpu.VMEM((HEADS, 2, POS), BF16),
            pltpu.VMEM((72, 4, D), BF16),
            pltpu.VMEM((D, 3 * D), BF16),
            pltpu.VMEM((D, D), BF16),
            pltpu.VMEM((D,), F32),
            pltpu.VMEM((D,), F32),
            pltpu.SemaphoreType.DMA((7,)),
            pltpu.VMEM((288, D), F32),
            pltpu.VMEM((8, CHUNKS * 128), I32),
            pltpu.VMEM((168, 128), I32),
            pltpu.VMEM((168, 128), I32),
            pltpu.VMEM((8, WIN, 128), I32),
            pltpu.VMEM((8, 192, 128), I32),
            pltpu.VMEM((288, D), F32),
            pltpu.VMEM((2, 256, D), BF16),
            pltpu.VMEM((2, 256, D), BF16),
            pltpu.VMEM((288, D), BF16),
        ],
        compiler_params=pltpu.CompilerParams(vmem_limit_bytes=WIDE),
        cost_estimate=cost(10**9, 3 * 10**6),
        name="first_block",
    )(
        position_index,
        bias_first.transpose(0, 2, 1, 3).reshape(HEADS, 2, POS),
        tokens.transpose(1, 2, 0, 3).reshape(72, 4, D),
        qkv_first, proj_first, gain_first, gain_second,
    )

    bias_shapes = (
        jax.ShapeDtypeStruct((2, 8, 80, 128), I32),
        jax.ShapeDtypeStruct((2, 8, 128, 128), I32),
    )
    bias_scratch = [
        pltpu.VMEM((2, 8, CHUNKS * 128), I32),
        pltpu.VMEM((2, 96, 128), I32),
        pltpu.VMEM((2, 96, 128), I32),
    ]
    from_west = shift(east, "lon", 1, True)
    size = lax.axis_size("lon")
    inner = [(i, i - 1) for i in range(size) if 0 < i % part < part - 1]
    seam = [(i, (i - 1) % size) for i in range(size) if i % part in (0, part - 1)]
    from_east = lax.ppermute(west, "lon", inner)
    before, west = lax.optimization_barrier((before, west))
    main, tail = pl.pallas_call(
        early_kernel,
        out_shape=bias_shapes,
        in_specs=[SMEM, VMEM, VMEM, VMEM],
        out_specs=(VMEM, VMEM),
        scratch_shapes=bias_scratch,
        compiler_params=params,
        cost_estimate=cost(10**6, 10**5),
        name="early_bias",
    )(where, position_index, table, before)
    main, tail, west = lax.optimization_barrier((main, tail, west))
    from_seam = lax.ppermute(west, "lon", seam)
    main, tail = pl.pallas_call(
        late_kernel,
        out_shape=bias_shapes,
        in_specs=[SMEM] + [VMEM] * 5,
        out_specs=(VMEM, VMEM),
        scratch_shapes=bias_scratch,
        compiler_params=params,
        cost_estimate=cost(10**9, 10**7),
        name="late_bias",
    )(where, position_index, table, before, main, tail)

    pieces = jax.ShapeDtypeStruct((4, 72, D), BF16)
    up, down = pl.pallas_call(
        stack_kernel,
        out_shape=(pieces, pieces),
        in_specs=[SMEM] + [VMEM] * 5 + [ANY],
        out_specs=(VMEM, VMEM),
        compiler_params=pltpu.CompilerParams(vmem_limit_bytes=4 * 1024 * 1024),
        cost_estimate=cost(10**5, 10**6),
        name="stack_pieces",
    )(where, west, east, from_west, from_east, from_seam, main)
    south = shift(up, "lat", -1, False)
    north = shift(down, "lat", 1, False)

    query, near = pl.pallas_call(
        near_kernel,
        out_shape=(jax.ShapeDtypeStruct((320, D), F32), jax.ShapeDtypeStruct((576, 2 * D), F32)),
        in_specs=[VMEM] * 3,
        out_specs=(VMEM, VMEM),
        scratch_shapes=[pltpu.VMEM((4, 160, D), F32), pltpu.VMEM((576, D), BF16)],
        compiler_params=params,
        cost_estimate=cost(10**9, 10**7),
        name="near_half",
    )(up, down, qkv_second)

    edges = jnp.stack([lat > 0, lat < last]).astype(I32)
    out = pl.pallas_call(
        second_kernel,
        out_shape=jax.ShapeDtypeStruct((72, 4, D), BF16),
        in_specs=[SMEM] + [VMEM] * 9,
        out_specs=VMEM,
        scratch_shapes=[
            pltpu.VMEM((4, 160, D), F32),
            pltpu.VMEM((576, D), BF16),
            pltpu.VMEM((288, D), F32),
            pltpu.VMEM((8, 256, D), BF16),
            pltpu.VMEM((8, 256, D), BF16),
            pltpu.VMEM((320, D), F32),
        ],
        compiler_params=params,
        cost_estimate=cost(10**9, 5 * 10**6),
        name="second_block",
    )(edges, first, query, near, north, south, qkv_second, proj_second, main, tail)
    return out.reshape(6, 12, 4, D).transpose(2, 0, 1, 3)


def solution(mesh):
    return jax.shard_map(
        shards,
        mesh=mesh,
        in_specs=(
            P(None, "lat", "lon", None), P(), P(), P(), P(),
            P("lat", None, None, None), P(), P(), P(), P("lat", None, None, None),
        ),
        out_specs=P(None, "lat", "lon", None),
        check_vma=False,
    )
```
